128 devices in a mesh: dp: 8 (over x, y_hi), head: 16 (over y_lo, z, core).
Axes of the slice: x: 4, y: 4 (y_hi: 2, y_lo: 2; y = y_hi * 2 + y_lo), z: 4, core: 2. Of those that a mesh axis runs over, the one named last changes fastest.
Arguments:
- inputs: bfloat16 [2048, 8192], P(('dp', 'head')), may hold values from -6 to 6
- gain: float32 [8192], replicated, may hold values from 0.1 to 1.9
- doc_ids: int32 [8, 256], P('dp'), may hold values from 0 to 3, never falling along the last dimension, each value on 1 to 128 neighbouring positions
- w_query: bfloat16 [8192, 8192], P(None, 'head'), may hold values from -0.0625 to 0.0625
- w_key: bfloat16 [8192, 1024], P(None, 'head'), may hold values from -0.0625 to 0.0625
- w_value: bfloat16 [8192, 1024], P(None, 'head'), may hold values from -0.0625 to 0.0625
- w_out: bfloat16 [8192, 8192], P('head'), may hold values from -0.0625 to 0.0625
- grad_out: bfloat16 [2048, 8192], P(('dp', 'head')), may hold values from -6 to 6
Outputs:
- outputs: bfloat16 [2048, 8192], P(('dp', 'head'))
- grad_in: bfloat16 [2048, 8192], P(('dp', 'head'))
- grad_gain: float32 [8192], replicated
- grad_wq: bfloat16 [8192, 8192], P('dp', 'head')
- grad_wk: bfloat16 [8192, 1024], P('dp', 'head')
- grad_wv: bfloat16 [8192, 1024], P('dp', 'head')
- grad_wo: bfloat16 [8192, 8192], P('head', 'dp')
The draws below stay inside these ranges and needn't reach their ends.
Inputs may be any that keep to these rules, and one draw needn't show every extreme that they name: `doc_ids`: document numbers never fall along a sequence; every document holds 1 to 128 tokens and one holds exactly 128.
All inputs are finite; a program needn't handle non-finite values.
Results may differ from the reference program's by a relative error of at most 0.03.
Values may be sent and summed in bfloat16 or wider, within the bound.
A program may use at most 128 MiB of HBM per device.

```python
import math
import jax
import jax.numpy as jnp
import numpy as np
from jax import lax

D = 8192
HD = 128
SEQ = 256
DOCS = 4
HQ = 64
KVH = 8
TOKENS = 2048
N_DP = 8
N_HEAD = 16


def block_levels(key, dims, pieces, least, high):
    def one(dim, blocks):
        heights = jax.random.uniform(jax.random.fold_in(jax.random.fold_in(key, 6), dim), (blocks,), jnp.float32, least / len(pieces), high / len(pieces))
        return jnp.repeat(jnp.exp(heights), dims[dim] // blocks).reshape((-1,) + (1,) * (len(dims) - dim - 1))

    level = one(*pieces[0])
    for cut in pieces[1:]:
        level = level * one(*cut)
    return level


def length_profile(count, total, most, skew):
    portions = [(1 << 20) // math.isqrt(grade ** skew) + 1 for grade in range(2, count + 1)]
    spare, counts = total - most - (count - 1), [1] * (count - 1)
    while spare > 0:
        free = [i for i in range(count - 1) if counts[i] < most]
        whole, budget = sum([portions[i] for i in free]), spare
        for i in free:
            addition = min(most - counts[i], max(1, budget * portions[i] // whole), spare)
            counts[i] = counts[i] + addition
            spare = spare - addition
    return np.array([most] + counts)


def uneven_parts(key, amount, total, most, lean):
    if amount == 2:
        one = jax.random.randint(key, (), max(1, total - most), min(most, total - 1) + 1)
        return jnp.stack([one, total - one])
    lengths = jnp.asarray(length_profile(amount, total, most, lean), jnp.int32)
    couples = (amount - 1) // 2
    source_of, sink = lengths[1:1 + 2 * couples:2], lengths[2:2 + 2 * couples:2]
    room = jnp.minimum(source_of - 1, most - sink)
    shifted = jax.random.randint(jax.random.fold_in(key, 1), (couples,), 0, 1 << 20) % (room + 1)
    lengths = lengths.at[1:1 + 2 * couples:2].set(source_of - shifted).at[2:2 + 2 * couples:2].set(sink + shifted)
    return lengths[jax.random.permutation(jax.random.fold_in(key, 2), amount)]


def bell_draw(stream_key, shape, spread, most, shards=(), held_as=jnp.bfloat16):
    array = spread * jax.random.normal(stream_key, shape, jnp.float32)
    if shards:
        array = array * block_levels(stream_key, shape, shards, -0.22, 0.18)
    return jnp.clip(array, -most, most).astype(held_as)


def setup_inputs(seed: int = 0) -> dict:
    streams_of = jax.random.split(jax.random.key(seed), 9)
    inputs = bell_draw(streams_of[0], (TOKENS, D), 1.0, 6.0, ((0, 128),))
    gain = jnp.clip(1.0 + 0.18 * jax.random.normal(streams_of[1], (D,), jnp.float32), 0.1, 1.9)
    doc_ids = jax.vmap(lambda own: jnp.searchsorted(jnp.cumsum(uneven_parts(own, DOCS, SEQ, SEQ // 2, 1)), jnp.arange(SEQ), side="right"))(jax.random.split(streams_of[2], N_DP)).reshape((N_DP, SEQ)).astype(jnp.int32)
    w_query = bell_draw(streams_of[3], (D, HQ * HD), D ** -0.5, 0.0625, ((1, 16),))
    w_key = bell_draw(streams_of[4], (D, KVH * HD), D ** -0.5, 0.0625, ((1, 16),))
    w_value = bell_draw(streams_of[5], (D, KVH * HD), D ** -0.5, 0.0625, ((1, 16),))
    w_out = bell_draw(streams_of[6], (HQ * HD, D), (HQ * HD) ** -0.5, 0.0625, ((0, 16),))
    grad_out = bell_draw(streams_of[7], (TOKENS, D), 1.0, 6.0, ((0, 128),))
    return {"inputs": inputs, "gain": gain, "doc_ids": doc_ids, "w_query": w_query, "w_key": w_key, "w_value": w_value, "w_out": w_out, "grad_out": grad_out}


EPSILON = 1e-05
THETA = 500000.0

def rotate(values):
    half_dim = values.shape[-1] // 2
    return jnp.concatenate([-values[..., half_dim:], values[..., :half_dim]], axis=-1)

def rotate_back(values):
    half_dim = values.shape[-1] // 2
    return jnp.concatenate([values[..., half_dim:], -values[..., :half_dim]], axis=-1)

def to_low(values):
    return lax.optimization_barrier(values.astype(jnp.bfloat16))

def tables(documents, head_dim):
    length = documents.shape[0]
    indices = jnp.arange(length, dtype=jnp.int32)
    starts = jnp.concatenate([jnp.ones((1,), dtype=bool), documents[1:] != documents[:-1]])
    first_index = lax.cummax(jnp.where(starts, indices, 0), axis=0)
    position = (indices - first_index).astype(jnp.float32)
    exponent = jnp.arange(head_dim // 2, dtype=jnp.float32) * (2.0 / head_dim)
    frequency = THETA ** (-exponent)
    angles = position[:, None] * frequency[None, :]
    cosine_table = jnp.concatenate([jnp.cos(angles)] * 2, axis=-1)
    sine_table = jnp.concatenate([jnp.sin(angles)] * 2, axis=-1)
    allowed = (documents[:, None] == documents[None, :]) & (indices[:, None] >= indices[None, :])
    return (cosine_table, sine_table, allowed)

def reference(inputs, gain, doc_ids, w_query, w_key, w_value, w_out, grad_out):
    score_scale = HD ** (-0.5)
    group_heads = HQ // N_HEAD
    half_dim = HD // 2
    group_cols = group_heads * HD
    query_groups = w_query.reshape(D, N_HEAD, group_cols).astype(jnp.float32)
    key_groups = w_key.reshape(D, N_HEAD, half_dim).astype(jnp.float32)
    value_groups = w_value.reshape(D, N_HEAD, half_dim).astype(jnp.float32)
    out_groups = w_out.reshape(N_HEAD, group_cols, D).astype(jnp.float32)

    def one_sequence(running, seq_items):
        sum_query, sum_pair, sum_out = running
        block_in, block_grad, documents = seq_items
        cosine_table, sine_table, allowed = tables(documents, HD)
        cosine_wide = cosine_table[:, None, :]
        sine_wide = sine_table[:, None, :]
        input_wide = block_in.astype(jnp.float32)
        inverse_rms = lax.rsqrt(lax.optimization_barrier(jnp.mean(input_wide * input_wide, axis=-1, keepdims=True)) + EPSILON)
        normed = (input_wide * inverse_rms * gain).astype(jnp.bfloat16)
        query_pre = jnp.dot(normed, w_query, preferred_element_type=jnp.float32).astype(jnp.bfloat16)
        key_pre = jnp.dot(normed, w_key, preferred_element_type=jnp.float32).astype(jnp.bfloat16)
        values = jnp.dot(normed, w_value, preferred_element_type=jnp.float32).astype(jnp.bfloat16)
        query_wide = query_pre.astype(jnp.float32).reshape(SEQ, HQ, HD)
        key_wide = key_pre.astype(jnp.float32).reshape(SEQ, KVH, HD)
        queries = (query_wide * cosine_wide + rotate(query_wide) * sine_wide).astype(jnp.bfloat16)
        key_rows = (key_wide * cosine_wide + rotate(key_wide) * sine_wide).astype(jnp.bfloat16)
        every_key = jnp.repeat(key_rows, HQ // KVH, axis=1).astype(jnp.float32)
        every_value = jnp.repeat(values.reshape(SEQ, KVH, HD), HQ // KVH, axis=1).astype(jnp.float32)
        scores = jnp.einsum('qhd,khd->hqk', queries.astype(jnp.float32), every_key) * score_scale
        scores = jnp.where(allowed[None], scores, -1e+30)
        attn_probs = jax.nn.softmax(scores, axis=-1)
        probs_low = attn_probs.astype(jnp.bfloat16)
        attended = jnp.einsum('hqk,khd->qhd', probs_low.astype(jnp.float32), every_value).astype(jnp.bfloat16)
        attended_flat = attended.reshape(SEQ, HQ * HD)
        out_parts = jnp.einsum('sgc,gcd->gsd', attended_flat.reshape(SEQ, N_HEAD, group_cols).astype(jnp.float32), out_groups)
        attn_sum = lax.optimization_barrier(jnp.sum(to_low(out_parts).astype(jnp.float32), axis=0))
        outputs = (input_wide + attn_sum).astype(jnp.bfloat16)
        grad_wide = block_grad.astype(jnp.float32)
        grad_att = jnp.dot(block_grad, w_out.T, preferred_element_type=jnp.float32).astype(jnp.bfloat16)
        grad_heads = grad_att.astype(jnp.float32).reshape(SEQ, HQ, HD)
        grad_probs = jnp.einsum('qhd,khd->hqk', grad_heads, every_value)
        row_delta = lax.optimization_barrier(jnp.sum(attn_probs * grad_probs, axis=-1, keepdims=True))
        grad_scores = (attn_probs * (grad_probs - row_delta)).astype(jnp.bfloat16).astype(jnp.float32)
        grad_query = jnp.einsum('hqk,khd->qhd', grad_scores, every_key) * score_scale
        query_raw = (grad_query * cosine_wide + rotate_back(grad_query * sine_wide)).astype(jnp.bfloat16)
        key_heads = jnp.einsum('hqk,qhd->khd', grad_scores, queries.astype(jnp.float32)) * score_scale
        key_sum = key_heads.reshape(SEQ, N_HEAD, group_heads, HD).sum(axis=2)
        key_group = to_low(key_sum * cosine_wide + rotate_back(key_sum * sine_wide))
        value_heads = jnp.einsum('hqk,qhd->khd', probs_low.astype(jnp.float32), grad_heads)
        value_group = to_low(value_heads.reshape(SEQ, N_HEAD, group_heads, HD).sum(axis=2))
        key_pair = (key_group[:, 0::2].astype(jnp.float32) + key_group[:, 1::2].astype(jnp.float32)).astype(jnp.bfloat16)
        value_pair = (value_group[:, 0::2].astype(jnp.float32) + value_group[:, 1::2].astype(jnp.float32)).astype(jnp.bfloat16)
        query_flat = query_raw.reshape(SEQ, N_HEAD, group_cols).astype(jnp.float32)
        key_halves = key_pair.reshape(SEQ, N_HEAD, half_dim).astype(jnp.float32)
        value_halves = value_pair.reshape(SEQ, N_HEAD, half_dim).astype(jnp.float32)
        in_parts = jnp.einsum('sgc,dgc->gsd', query_flat, query_groups)
        in_parts = in_parts + jnp.einsum('sgc,dgc->gsd', key_halves, key_groups)
        in_parts = in_parts + jnp.einsum('sgc,dgc->gsd', value_halves, value_groups)
        grad_normed = lax.optimization_barrier(jnp.sum(to_low(in_parts).astype(jnp.float32), axis=0))
        gain_part = lax.optimization_barrier(jnp.sum(grad_normed * input_wide * inverse_rms, axis=0))
        scaled = grad_normed * gain
        grad_in = (grad_wide + inverse_rms * scaled - input_wide * inverse_rms ** 3 * lax.optimization_barrier(jnp.mean(scaled * input_wide, axis=-1, keepdims=True))).astype(jnp.bfloat16)
        query_term = jnp.dot(normed.T, query_raw.reshape(SEQ, HQ * HD), preferred_element_type=jnp.float32)
        sum_query = sum_query + to_low(query_term).astype(jnp.float32)
        pair_cols = jnp.concatenate([key_pair.reshape(SEQ, KVH * HD), value_pair.reshape(SEQ, KVH * HD)], axis=1)
        pair_term = jnp.dot(normed.T, pair_cols, preferred_element_type=jnp.float32)
        sum_pair = sum_pair + to_low(pair_term).astype(jnp.float32)
        out_term = jnp.dot(attended_flat.T, block_grad, preferred_element_type=jnp.float32)
        sum_out = sum_out + to_low(out_term).astype(jnp.float32)
        return ((sum_query, sum_pair, sum_out), (outputs, grad_in, gain_part))
    start_sums = (jnp.zeros((D, HQ * HD), jnp.float32), jnp.zeros((D, 2 * KVH * HD), jnp.float32), jnp.zeros((HQ * HD, D), jnp.float32))
    seq_items = (inputs.reshape(N_DP, SEQ, D), grad_out.reshape(N_DP, SEQ, D), doc_ids)
    sums, stacked = lax.scan(one_sequence, start_sums, seq_items)
    sum_query, sum_pair, sum_out = sums
    outputs, grad_in, gain_parts = stacked
    grad_gain = lax.optimization_barrier(jnp.sum(gain_parts, axis=0))
    return (outputs.reshape(N_DP * SEQ, D), grad_in.reshape(N_DP * SEQ, D), grad_gain, sum_query.astype(jnp.bfloat16), sum_pair[:, :KVH * HD].astype(jnp.bfloat16), sum_pair[:, KVH * HD:].astype(jnp.bfloat16), sum_out.astype(jnp.bfloat16))
```

```python
import functools

import jax
import jax.numpy as jnp
from jax import lax
from jax.experimental import pallas as pl
from jax.experimental.pallas import tpu as pltpu
from jax.sharding import PartitionSpec as P

EPSILON = 1e-05
THETA = 500000.0
MESH = pl.DeviceIdType.MESH
BF = jnp.bfloat16
F32 = jnp.float32

ROWS = 16
CHUNKS = 8
CHUNK = 1024
SEQ = 256
HEADS = 4
HD = 128


def device(x, yh, yl, z, c):
    return (x * 2 + yh, (yl * 4 + z) * 2 + c)


def dot(a, b):
    return jnp.dot(a, b, preferred_element_type=F32)


def dot_nt(a, b):
    return lax.dot_general(a, b, (((1,), (1,)), ((), ())), preferred_element_type=F32)


def dot_tn(a, b):
    return lax.dot_general(a, b, (((0,), (0,)), ((), ())), preferred_element_type=F32)


class Link:
    def __init__(self, send, recv):
        self.send, self.recv, self.started = send, recv, []

    def copy(self, k, src, dst, to):
        return pltpu.make_async_remote_copy(
            src_ref=src,
            dst_ref=dst,
            send_sem=self.send.at[k],
            recv_sem=self.recv.at[k],
            device_id=to,
            device_id_type=MESH,
        )

    def start(self, k, src, dst, to):
        cp = self.copy(k, src, dst, to)
        cp.start()
        self.started.append(cp)

    def arrived(self, k, dst, to):
        self.copy(k, dst, dst, to).wait_recv()

    def sent(self):
        for cp in self.started:
            cp.wait_send()
        self.started = []


class Gather:
    def __init__(self, link, slot, half, place, pair, ring, core):
        self.link, self.slot, self.half = link, slot, half
        self.p, self.r = place
        self.pair_dev, self.core_dev = pair, core
        self.next_dev, self.prev_dev = ring
        self.q = 1 - self.p
        self.nxt, self.prv, self.far = (self.r + 1) % 4, (self.r + 3) % 4, (self.r + 2) % 4
        self.shared = []

    def put(self, k, p, r, to):
        ref = self.slot(p, r)
        self.link.start(k, ref, ref, to)

    def put_half(self, k, p, r, h, to):
        ref = self.half(p, r, h)
        self.link.start(k, ref, ref, to)

    def got(self, k, p, r):
        self.link.arrived(k, self.slot(p, r), self.pair_dev)

    def got_half(self, k, p, r, h):
        self.link.arrived(k, self.half(p, r, h), self.pair_dev)

    def share(self, p, r):
        if self.core_dev is not None:
            self.put(9 + len(self.shared), p, r, self.core_dev)
            self.shared.append((p, r))

    def start_pair(self):
        self.put(0, self.p, self.r, self.pair_dev)

    def start_ring(self):
        self.put(1, self.p, self.r, self.next_dev)
        self.put(2, self.p, self.r, self.prev_dev)
        self.share(self.p, self.r)

    def on_pair(self):
        self.got(0, self.q, self.r)
        self.put(3, self.q, self.r, self.next_dev)
        self.put(4, self.q, self.r, self.prev_dev)
        self.share(self.q, self.r)

    def on_ring(self, p, base, k):
        self.got(base, p, self.prv)
        self.put_half(k, p, self.prv, 0, self.next_dev)
        self.share(p, self.prv)
        self.got(base + 1, p, self.nxt)
        self.put_half(k + 1, p, self.nxt, 1, self.prev_dev)
        self.share(p, self.nxt)

    def on_ring_own(self):
        self.on_ring(self.p, 1, 5)

    def on_ring_pair(self):
        self.on_ring(self.q, 3, 7)

    def on_far(self):
        for p, k in ((self.p, 5), (self.q, 7)):
            self.got_half(k, p, self.far, 0)
            self.got_half(k + 1, p, self.far, 1)
            self.share(p, self.far)

    def last_ring(self):
        self.got(1, self.p, self.prv)
        self.put_half(5, self.p, self.prv, 0, self.next_dev)
        self.put(3, self.p, self.prv, self.pair_dev)
        self.share(self.p, self.prv)
        self.got(2, self.p, self.nxt)
        self.put_half(6, self.p, self.nxt, 1, self.prev_dev)
        self.put(4, self.p, self.nxt, self.pair_dev)
        self.share(self.p, self.nxt)

    def last_far(self):
        self.got_half(5, self.p, self.far, 0)
        self.got_half(6, self.p, self.far, 1)
        self.put(7, self.p, self.far, self.pair_dev)
        self.share(self.p, self.far)

    def last_pair(self):
        for k, r in ((0, self.r), (3, self.prv), (4, self.nxt), (7, self.far)):
            self.got(k, self.q, r)
            self.share(self.q, r)

    def done(self, other_slot=None):
        for i, (p, r) in enumerate(self.shared):
            self.link.arrived(9 + i, other_slot(p, r), self.pair_dev)

    def sent(self):
        self.link.sent()


class Scatter:
    def __init__(self, link, parts, bufs, place, devs):
        self.link, self.parts = link, parts
        self.from_core, self.from_prev_half, self.from_next_half, self.from_prev, self.from_next, self.from_pair = bufs
        self.yl, self.z, self.c = place
        self.core_dev, self.pair_dev, self.next_dev, self.prev_dev = devs
        self.nxt, self.prv, self.far = (self.z + 1) % 4, (self.z + 3) % 4, (self.z + 2) % 4

    def give_core(self, ch):
        self.link.copy(
            ch, self.parts.at[ch, :, :, 1 - self.c], self.from_core.at[ch], self.core_dev
        ).start()

    def add_core(self):
        def step(ch, carry):
            self.link.copy(
                ch, self.parts.at[ch, :, :, 1 - self.c], self.from_core.at[ch], self.core_dev
            ).wait()
            own = self.parts[ch, :, :, self.c].astype(F32)
            self.parts[ch, :, :, self.c] = (own + self.from_core[ch].astype(F32)).astype(BF)
            return carry

        lax.fori_loop(0, CHUNKS, step, 0)

    def half(self, z, h):
        return self.parts.at[4 * h : 4 * h + 4, :, z, self.c]

    def start(self):
        link = self.link
        link.start(8, self.half(self.far, 0), self.from_prev_half, self.next_dev)
        link.start(9, self.half(self.far, 1), self.from_next_half, self.prev_dev)
        link.start(10, self.half(self.nxt, 1), self.from_prev.at[4:8], self.next_dev)
        link.start(11, self.half(self.prv, 0), self.from_next.at[0:4], self.prev_dev)

    def middle(self):
        link = self.link
        link.arrived(8, self.from_prev_half, self.pair_dev)
        for ch in range(4):
            mine = self.parts[ch, :, self.nxt, self.c].astype(F32)
            self.parts[ch, :, self.nxt, self.c] = (mine + self.from_prev_half[ch].astype(F32)).astype(BF)
        link.start(12, self.half(self.nxt, 0), self.from_prev.at[0:4], self.next_dev)
        link.arrived(9, self.from_next_half, self.pair_dev)
        for ch in range(4):
            mine = self.parts[4 + ch, :, self.prv, self.c].astype(F32)
            self.parts[4 + ch, :, self.prv, self.c] = (mine + self.from_next_half[ch].astype(F32)).astype(BF)
        link.start(13, self.half(self.prv, 1), self.from_next.at[4:8], self.prev_dev)

    def to_pair(self):
        link = self.link
        link.arrived(10, self.from_prev.at[4:8], self.pair_dev)
        link.arrived(11, self.from_next.at[0:4], self.pair_dev)
        for k, h in ((12, 0), (13, 1)):
            buf = self.from_prev if h == 0 else self.from_next
            link.arrived(k, buf.at[4 * h : 4 * h + 4], self.pair_dev)
            for ch in range(4 * h, 4 * h + 4):
                total = (
                    self.parts[ch, :, self.z, self.c].astype(F32)
                    + self.from_prev[ch].astype(F32)
                    + self.from_next[ch].astype(F32)
                )
                self.parts[ch, :, self.z, self.c] = total.astype(BF)
            link.start(
                14 + h,
                self.parts.at[4 * h : 4 * h + 4, 1 - self.yl, self.z, self.c],
                self.from_pair.at[4 * h : 4 * h + 4],
                self.pair_dev,
            )

    def arrived(self, h):
        self.link.arrived(14 + h, self.from_pair.at[4 * h : 4 * h + 4], self.pair_dev)

    def chunk(self, ch):
        return self.parts[ch, self.yl, self.z, self.c].astype(F32) + self.from_pair[ch].astype(F32)

    def sent(self):
        self.link.sent()


def layer(
    inputs_ref, gain_ref, doc_row_ref, doc_col_ref, freq_ref, wq_hbm, wkv_hbm, wo_hbm, gout_ref,
    out_ref, gin_ref, ggain_ref, gwq_ref, gwk_ref, gwv_ref, gwo_ref,
    xs, gs, nc, gc, wq, wkv, wo, att, qkv, acc, kvh, kvg, qh, probs,
    rs0, rs1, rs2, rs3, rs4, rs5, rt0, rt1, rt2, rt3, rt4, rt5,
    ga0, ga1, ga2,
    x_s, x_r, g_s, g_r, nc_s, nc_r, gc_s, gc_r, at_s, at_r, qk_s, qk_r, ro_s, ro_r, rg_s, rg_r,
    tn_s, tn_r, tg_s, tg_r, kv_s, kv_r, ga_s, ga_r, w_sem,
):
    dp, head = lax.axis_index("dp"), lax.axis_index("head")
    x, yh = dp // 2, dp % 2
    yl, z, c = head // 8, (head // 2) % 4, head % 2
    core_dev = device(x, yh, yl, z, 1 - c)
    pair_dev = device(x, yh, 1 - yl, z, c)
    z_dev = [device(x, yh, yl, (z + k) % 4, c) for k in range(4)]
    dp_devs = [((dp + k) % 8, head) for k in range(1, 8)]
    x_dev = [device((x + k) % 4, yh, yl, z, c) for k in range(4)]
    yh_dev = device(x, 1 - yh, yl, z, c)
    diag_dev = device(x, yh, 1 - yl, z, 1 - c)

    weights = [
        pltpu.make_async_copy(wq_hbm, wq, w_sem.at[0]),
        pltpu.make_async_copy(wkv_hbm, wkv, w_sem.at[1]),
        pltpu.make_async_copy(wo_hbm, wo, w_sem.at[2]),
    ]
    for cp in weights:
        cp.start()

    barrier = pltpu.get_barrier_semaphore()
    partners = [core_dev, pair_dev, diag_dev] + z_dev[1:] + dp_devs
    for to in partners:
        pl.semaphore_signal(barrier, inc=1, device_id=to, device_id_type=MESH)

    square = jnp.zeros((ROWS, 1), F32)
    for ch in range(CHUNKS):
        part = inputs_ref[:, ch * CHUNK : (ch + 1) * CHUNK].astype(F32)
        square += jnp.sum(part * part, axis=-1, keepdims=True)
    inverse_rms = lax.rsqrt(square * (1.0 / (CHUNKS * CHUNK)) + EPSILON)
    for ch in range(CHUNKS):
        cols = slice(ch * CHUNK, (ch + 1) * CHUNK)
        part = inputs_ref[:, cols].astype(F32)
        xs[ch, yl, z, c] = (part * inverse_rms * gain_ref[:, cols]).astype(BF)
        gs[ch, yl, z, c] = gout_ref[:, cols]
    nc[dp, yl, z, c] = xs[dp, yl, z, c]
    gc[dp, yl, z, c] = gs[dp, yl, z, c]

    pl.semaphore_wait(barrier, len(partners))

    def head_gather(buf, send, recv):
        return Gather(
            Link(send, recv),
            lambda p, r: buf.at[:, p, r, c],
            lambda p, r, h: buf.at[4 * h : 4 * h + 4, p, r, c],
            (yl, z), pair_dev, (z_dev[1], z_dev[3]), core_dev,
        )

    def other_core(buf):
        return lambda p, r: buf.at[:, p, r, 1 - c]

    def dp_gather(buf, send, recv):
        return Gather(
            Link(send, recv),
            lambda p, r: buf.at[r, p],
            lambda p, r, h: buf.at[r, p, 128 * h : 128 * h + 128],
            (yh, x), yh_dev, (x_dev[1], x_dev[3]), None,
        )

    gx, gg = head_gather(xs, x_s, x_r), head_gather(gs, g_s, g_r)
    gnc, ggc = head_gather(nc, nc_s, nc_r), head_gather(gc, gc_s, gc_r)
    gat, gqk = dp_gather(att, at_s, at_r), dp_gather(qkv, qk_s, qk_r)
    devs = (core_dev, pair_dev, z_dev[1], z_dev[3])
    ro = Scatter(Link(ro_s, ro_r), xs, (rs0, rs1, rs2, rs3, rs4, rs5), (yl, z, c), devs)
    rg = Scatter(Link(rg_s, rg_r), gs, (rt0, rt1, rt2, rt3, rt4, rt5), (yl, z, c), devs)

    gx.start_ring()
    gx.start_pair()
    gg.start_pair()
    tiny_n, tiny_g = Link(tn_s, tn_r), Link(tg_s, tg_r)
    for link, src, dst in ((tiny_n, xs, nc), (tiny_g, gs, gc)):
        for k in range(1, 8):
            to = (dp + k) % 8
            link.start(k - 1, src.at[to, yl, z, c], dst.at[dp, yl, z, c], (to, head))

    row_index = lax.broadcasted_iota(jnp.int32, (SEQ, SEQ), 0)
    col_index = lax.broadcasted_iota(jnp.int32, (SEQ, SEQ), 1)
    same = doc_col_ref[...] == doc_row_ref[...]
    allowed = same & (col_index <= row_index)
    position = jnp.sum(jnp.where(allowed, 1.0, 0.0), axis=-1, keepdims=True) - 1.0
    angles = position * freq_ref[...]
    cosine, sine = jnp.cos(angles), jnp.sin(angles)
    lane = lax.broadcasted_iota(jnp.int32, (SEQ, HD), 1)
    low_half = lane < HD // 2
    sine_turn = jnp.where(low_half, -sine, sine)

    def rope(u):
        return u * cosine + pltpu.roll(u, HD // 2, 1) * sine_turn

    def rope_back(g):
        turned = pltpu.roll(g * sine, HD // 2, 1)
        return g * cosine + jnp.where(low_half, turned, -turned)

    gx.on_pair()
    gx.on_ring_own()
    gx.on_ring_pair()
    gg.start_ring()
    gg.on_pair()
    gx.on_far()
    gx.done(other_core(xs))

    weights[0].wait()
    weights[1].wait()

    def project(ch, carry):
        block = xs[ch].reshape(SEQ, CHUNK)
        rows = pl.ds(pl.multiple_of(ch * CHUNK, CHUNK), CHUNK)
        acc[...] += dot(block, wq[rows, :])
        kvh_acc[...] += dot(block, wkv[rows, :])
        return carry

    kvh_acc = probs.at[0, :, 0:HD]
    acc[...] = jnp.zeros_like(acc)
    kvh_acc[...] = jnp.zeros((SEQ, HD), F32)
    lax.fori_loop(0, CHUNKS, project, 0)
    kvh[c] = kvh_acc[...].astype(BF)
    kv_link = Link(kv_s, kv_r)
    kv_link.start(0, kvh.at[c], kvh.at[c], core_dev)
    for h in range(HEADS):
        pre = acc[:, h * HD : (h + 1) * HD].astype(BF).astype(F32)
        qh[h] = rope(pre).astype(BF)
    gg.on_ring_own()
    gg.on_ring_pair()
    kv_link.arrived(0, kvh.at[1 - c], core_dev)
    first, second = kvh[0].astype(F32), kvh[1].astype(F32)
    key_pre = jnp.where(low_half, first, pltpu.roll(second, HD // 2, 1))
    values = jnp.where(low_half, pltpu.roll(first, HD // 2, 1), second).astype(BF)
    key_rows = rope(key_pre).astype(BF)
    score_scale = HD ** (-0.5)

    for h in range(HEADS):
        scores = dot_nt(qh[h], key_rows) * score_scale
        scores = jnp.where(allowed, scores, -1e30)
        top = jnp.max(scores, axis=-1, keepdims=True)
        e = jnp.exp(scores - top)
        p = e / jnp.sum(e, axis=-1, keepdims=True)
        probs[h] = p
        att[x, yh, :, h * HD : (h + 1) * HD] = dot(p.astype(BF), values).astype(BF)
    gat.start_ring()
    gat.start_pair()

    gx.sent()
    tiny_n.sent()
    weights[2].wait()
    wide = (2, 4, 2, ROWS, CHUNK)

    def project_out(ch, carry):
        cols = pl.ds(pl.multiple_of(ch * CHUNK, CHUNK), CHUNK)
        xs[ch] = dot(att[x, yh], wo[:, cols]).astype(BF).reshape(wide)
        ro.give_core(ch)
        return carry

    lax.fori_loop(0, CHUNKS, project_out, 0)
    gg.on_far()
    gg.done(other_core(gs))
    ro.add_core()
    ro.start()

    acc[...] = jnp.zeros_like(acc)

    def back_out(ch, carry):
        cols = pl.ds(pl.multiple_of(ch * CHUNK, CHUNK), CHUNK)
        acc[...] += dot_nt(gs[ch].reshape(SEQ, CHUNK), wo[:, cols])
        return carry

    lax.fori_loop(0, CHUNKS, back_out, 0)
    gat.on_pair()
    ro.middle()
    key_sum = jnp.zeros((SEQ, HD), F32)
    value_sum = jnp.zeros((SEQ, HD), F32)
    for h in range(HEADS):
        grad_att = acc[:, h * HD : (h + 1) * HD].astype(BF)
        p = probs[h]
        grad_probs = dot_nt(grad_att, values)
        delta = jnp.sum(p * grad_probs, axis=-1, keepdims=True)
        grad_scores = (p * (grad_probs - delta)).astype(BF)
        grad_query = dot(grad_scores, key_rows) * score_scale
        qkv[x, yh, :, h * HD : (h + 1) * HD] = rope_back(grad_query).astype(BF)
        key_sum += dot_tn(grad_scores, qh[h])
        value_sum += dot_tn(p.astype(BF), grad_att)
    kvg[c, 0] = rope_back(key_sum * score_scale).astype(BF)
    kvg[c, 1] = value_sum.astype(BF)
    kv_link.start(1, kvg.at[c], kvg.at[c], core_dev)
    gat.on_ring_own()
    gat.on_ring_pair()
    kv_link.arrived(1, kvg.at[1 - c], core_dev)
    key_pair = (kvg[0, 0].astype(F32) + kvg[1, 0].astype(F32)).astype(BF).astype(F32)
    value_pair = (kvg[0, 1].astype(F32) + kvg[1, 1].astype(F32)).astype(BF).astype(F32)
    even = jnp.where(low_half, key_pair, pltpu.roll(value_pair, HD // 2, 1))
    odd = jnp.where(low_half, pltpu.roll(key_pair, HD // 2, 1), value_pair)
    qkv[x, yh, :, HEADS * HD :] = jnp.where(c == 0, even, odd).astype(BF)
    gqk.start_ring()
    gqk.start_pair()

    gg.sent()
    tiny_g.sent()

    def back_in(ch, carry):
        rows = pl.ds(pl.multiple_of(ch * CHUNK, CHUNK), CHUNK)
        part = dot_nt(qkv[x, yh, :, : HEADS * HD], wq[rows, :])
        part += dot_nt(qkv[x, yh, :, HEADS * HD :], wkv[rows, :])
        gs[ch] = part.astype(BF).reshape(wide)
        rg.give_core(ch)
        return carry

    lax.fori_loop(0, CHUNKS, back_in, 0)
    ro.to_pair()
    rg.add_core()
    rg.start()

    for link, dst in ((tiny_n, nc), (tiny_g, gc)):
        for k in range(1, 8):
            link.arrived(k - 1, dst.at[(dp + 8 - k) % 8, yl, z, c], core_dev)
    gnc.start_ring()
    gnc.start_pair()
    ggc.start_ring()
    ggc.start_pair()
    gat.on_far()
    gqk.on_pair()
    rg.middle()
    gqk.on_ring_own()
    gqk.on_ring_pair()
    for h in range(2):
        ro.arrived(h)
        for ch in range(4 * h, 4 * h + 4):
            cols = slice(ch * CHUNK, (ch + 1) * CHUNK)
            out_ref[:, cols] = (inputs_ref[:, cols].astype(F32) + ro.chunk(ch)).astype(BF)
    gqk.on_far()
    rg.to_pair()
    gnc.last_ring()
    ggc.last_ring()

    mean = jnp.zeros((ROWS, 1), F32)
    gain_slot = yl * 2 + c
    for h in range(2):
        rg.arrived(h)
        for ch in range(4 * h, 4 * h + 4):
            cols = slice(ch * CHUNK, (ch + 1) * CHUNK)
            grad = rg.chunk(ch)
            part = inputs_ref[:, cols].astype(F32)
            ga0[gain_slot, ch : ch + 1] = jnp.sum(grad * part * inverse_rms, axis=0, keepdims=True)
            mean += jnp.sum(grad * gain_ref[:, cols] * part, axis=-1, keepdims=True)
    ga_link = Link(ga_s, ga_r)
    near = [(core_dev, yl * 2 + 1 - c), (pair_dev, (1 - yl) * 2 + c), (diag_dev, (1 - yl) * 2 + 1 - c)]
    for k, (to, _) in enumerate(near):
        ga_link.start(k, ga0.at[gain_slot], ga0.at[gain_slot], to)
    mean = mean * (1.0 / (CHUNKS * CHUNK)) * inverse_rms * inverse_rms * inverse_rms
    for ch in range(CHUNKS):
        cols = slice(ch * CHUNK, (ch + 1) * CHUNK)
        part = inputs_ref[:, cols].astype(F32)
        scaled = rg.chunk(ch) * gain_ref[:, cols]
        gin_ref[:, cols] = (gout_ref[:, cols].astype(F32) + inverse_rms * scaled - part * mean).astype(BF)
    gnc.last_far()
    ggc.last_far()
    for k, (_, slot) in enumerate(near):
        ga_link.arrived(k, ga0.at[slot], core_dev)
    ga1[z] = (ga0[0] + ga0[1]) + (ga0[2] + ga0[3])
    for k in range(1, 4):
        ga_link.start(2 + k, ga1.at[z], ga1.at[z], z_dev[k])

    gnc.last_pair()
    ggc.last_pair()
    for k in range(1, 4):
        ga_link.arrived(2 + k, ga1.at[(z + 4 - k) % 4], core_dev)
    ga2[dp] = (ga1[0] + ga1[1]) + (ga1[2] + ga1[3])
    for k in range(1, 8):
        ga_link.start(5 + k, ga2.at[dp], ga2.at[dp], ((dp + k) % 8, head))

    gnc.done(other_core(nc))
    total = None
    for s in range(8):
        term = dot_tn(nc[s].reshape(SEQ, CHUNK), qkv[s // 2, s % 2])
        total = term if total is None else total + term
    gwq_ref[...] = total[:, : HEADS * HD].astype(BF)
    gwk_ref[...] = total[:, HEADS * HD : HEADS * HD + HD // 2].astype(BF)
    gwv_ref[...] = total[:, HEADS * HD + HD // 2 :].astype(BF)
    ggc.done(other_core(gc))
    total = None
    for s in range(8):
        term = dot_tn(att[s // 2, s % 2], gc[s].reshape(SEQ, CHUNK))
        total = term if total is None else total + term
    gwo_ref[...] = total.astype(BF)

    for k in range(1, 8):
        ga_link.arrived(5 + k, ga2.at[(dp + 8 - k) % 8], core_dev)
    ggain_ref[...] = ((ga2[0] + ga2[1]) + (ga2[2] + ga2[3])) + ((ga2[4] + ga2[5]) + (ga2[6] + ga2[7]))

    for link in (gat, gqk, gnc, ggc, ro, rg, kv_link, ga_link):
        link.sent()


def per_device(inputs, gain, doc_ids, w_query, w_key, w_value, w_out, grad_out):
    w_kv = jnp.concatenate([w_key, w_value], axis=1)
    exponent = jnp.arange(HD // 2, dtype=F32) * (2.0 / HD)
    frequency = THETA ** (-exponent)
    frequency = jnp.concatenate([frequency, frequency])[None, :]
    vmem = pl.BlockSpec(memory_space=pltpu.VMEM)
    hbm = pl.BlockSpec(memory_space=pl.ANY)
    rows = (CHUNKS, 2, 4, 2, ROWS, CHUNK)
    half = (4, 2, ROWS, CHUNK)
    scatter = [
        pltpu.VMEM((CHUNKS, 2, 4, ROWS, CHUNK), BF),
        pltpu.VMEM(half, BF),
        pltpu.VMEM(half, BF),
        pltpu.VMEM((CHUNKS, 2, ROWS, CHUNK), BF),
        pltpu.VMEM((CHUNKS, 2, ROWS, CHUNK), BF),
        pltpu.VMEM((CHUNKS, ROWS, CHUNK), BF),
    ]
    dma = lambda n: [pltpu.SemaphoreType.DMA((n,))] * 2
    outs = pl.pallas_call(
        layer,
        out_shape=(
            jax.ShapeDtypeStruct((ROWS, CHUNKS * CHUNK), BF),
            jax.ShapeDtypeStruct((ROWS, CHUNKS * CHUNK), BF),
            jax.ShapeDtypeStruct((CHUNKS, CHUNK), F32),
            jax.ShapeDtypeStruct((CHUNK, HEADS * HD), BF),
            jax.ShapeDtypeStruct((CHUNK, HD // 2), BF),
            jax.ShapeDtypeStruct((CHUNK, HD // 2), BF),
            jax.ShapeDtypeStruct((HEADS * HD, CHUNK), BF),
        ),
        in_specs=[vmem] * 5 + [hbm] * 3 + [vmem],
        out_specs=[vmem] * 7,
        scratch_shapes=[
            pltpu.VMEM(rows, BF),
            pltpu.VMEM(rows, BF),
            pltpu.VMEM(rows, BF),
            pltpu.VMEM(rows, BF),
            pltpu.VMEM((CHUNKS * CHUNK, HEADS * HD), BF),
            pltpu.VMEM((CHUNKS * CHUNK, HD), BF),
            pltpu.VMEM((HEADS * HD, CHUNKS * CHUNK), BF),
            pltpu.VMEM((4, 2, SEQ, HEADS * HD), BF),
            pltpu.VMEM((4, 2, SEQ, HEADS * HD + HD), BF),
            pltpu.VMEM((SEQ, HEADS * HD), F32),
            pltpu.VMEM((2, SEQ, HD), BF),
            pltpu.VMEM((2, 2, SEQ, HD), BF),
            pltpu.VMEM((HEADS, SEQ, HD), BF),
            pltpu.VMEM((HEADS, SEQ, SEQ), F32),
        ]
        + scatter
        + scatter
        + [
            pltpu.VMEM((4, CHUNKS, CHUNK), F32),
            pltpu.VMEM((4, CHUNKS, CHUNK), F32),
            pltpu.VMEM((8, CHUNKS, CHUNK), F32),
        ]
        + dma(17) * 4
        + dma(9) * 2
        + dma(16) * 2
        + dma(7) * 2
        + dma(2)
        + dma(13)
        + [pltpu.SemaphoreType.DMA((3,))],
        compiler_params=pltpu.CompilerParams(
            collective_id=0, has_side_effects=True, vmem_limit_bytes=60 * 2**20
        ),
    )(
        inputs,
        gain[None, :],
        doc_ids,
        doc_ids.reshape(SEQ, 1),
        frequency,
        w_query,
        w_kv,
        w_out,
        grad_out,
    )
    out, gin, ggain, gwq, gwk, gwv, gwo = outs
    return (out, gin, ggain.reshape(-1), gwq, gwk, gwv, gwo)


def solution(mesh):
    return jax.shard_map(
        per_device,
        mesh=mesh,
        in_specs=(
            P(("dp", "head"), None),
            P(),
            P("dp", None),
            P(None, "head"),
            P(None, "head"),
            P(None, "head"),
            P("head", None),
            P(("dp", "head"), None),
        ),
        out_specs=(
            P(("dp", "head"), None),
            P(("dp", "head"), None),
            P(),
            P("dp", "head"),
            P("dp", "head"),
            P("dp", "head"),
            P("head", "dp"),
        ),
        check_vma=False,
    )
```

```python
import math

import jax
import jax.numpy as jnp
from jax import lax
from jax.experimental import pallas as pl
from jax.experimental.pallas import tpu as pltpu
from jax.sharding import PartitionSpec as P

EPSILON = 1e-05
LOG_THETA = math.log(500000.0)
MESH = pl.DeviceIdType.MESH
BF = jnp.bfloat16
F32 = jnp.float32

ROWS = 16
CHUNKS = 8
CHUNK = 1024
SEQ = 256
HEADS = 4
HD = 128


def device(x, yh, yl, z, c):
    return (x * 2 + yh, (yl * 4 + z) * 2 + c)


def dot(a, b):
    return jnp.dot(a, b, preferred_element_type=F32)


def dot_nt(a, b):
    return lax.dot_general(a, b, (((1,), (1,)), ((), ())), preferred_element_type=F32)


def dot_tn(a, b):
    return lax.dot_general(a, b, (((0,), (0,)), ((), ())), preferred_element_type=F32)


class Link:
    def __init__(self, send, recv):
        self.send, self.recv, self.started = send, recv, []

    def copy(self, k, src, dst, to):
        return pltpu.make_async_remote_copy(
            src_ref=src,
            dst_ref=dst,
            send_sem=self.send.at[k],
            recv_sem=self.recv.at[k],
            device_id=to,
            device_id_type=MESH,
        )

    def start(self, k, src, dst, to):
        cp = self.copy(k, src, dst, to)
        cp.start()
        self.started.append(cp)

    def arrived(self, k, dst, to):
        self.copy(k, dst, dst, to).wait_recv()

    def sent(self):
        for cp in self.started:
            cp.wait_send()
        self.started = []


class Gather:
    def __init__(self, link, slot, half, place, pair, ring, core):
        self.link, self.slot, self.half = link, slot, half
        self.p, self.r = place
        self.pair_dev, self.core_dev = pair, core
        self.next_dev, self.prev_dev = ring
        self.q = 1 - self.p
        self.nxt, self.prv, self.far = (self.r + 1) % 4, (self.r + 3) % 4, (self.r + 2) % 4
        self.shared = []

    def put(self, k, p, r, to):
        ref = self.slot(p, r)
        self.link.start(k, ref, ref, to)

    def put_half(self, k, p, r, h, to):
        ref = self.half(p, r, h)
        self.link.start(k, ref, ref, to)

    def got(self, k, p, r):
        self.link.arrived(k, self.slot(p, r), self.pair_dev)

    def got_half(self, k, p, r, h):
        self.link.arrived(k, self.half(p, r, h), self.pair_dev)

    def share(self, p, r):
        if self.core_dev is not None:
            self.put(9 + len(self.shared), p, r, self.core_dev)
            self.shared.append((p, r))

    def start_pair(self):
        self.put(0, self.p, self.r, self.pair_dev)

    def start_ring(self):
        self.put(1, self.p, self.r, self.next_dev)
        self.put(2, self.p, self.r, self.prev_dev)
        self.share(self.p, self.r)

    def on_pair(self):
        self.got(0, self.q, self.r)
        self.put(3, self.q, self.r, self.next_dev)
        self.put(4, self.q, self.r, self.prev_dev)
        self.share(self.q, self.r)

    def on_ring(self, p, base, k):
        self.got(base, p, self.prv)
        self.put_half(k, p, self.prv, 0, self.next_dev)
        self.share(p, self.prv)
        self.got(base + 1, p, self.nxt)
        self.put_half(k + 1, p, self.nxt, 1, self.prev_dev)
        self.share(p, self.nxt)

    def on_ring_own(self):
        self.on_ring(self.p, 1, 5)

    def on_ring_pair(self):
        self.on_ring(self.q, 3, 7)

    def on_far(self):
        for p, k in ((self.p, 5), (self.q, 7)):
            self.got_half(k, p, self.far, 0)
            self.got_half(k + 1, p, self.far, 1)
            self.share(p, self.far)

    def last_ring(self):
        self.got(1, self.p, self.prv)
        self.put_half(5, self.p, self.prv, 0, self.next_dev)
        self.put(3, self.p, self.prv, self.pair_dev)
        self.share(self.p, self.prv)
        self.got(2, self.p, self.nxt)
        self.put_half(6, self.p, self.nxt, 1, self.prev_dev)
        self.put(4, self.p, self.nxt, self.pair_dev)
        self.share(self.p, self.nxt)

    def last_far(self):
        self.got_half(5, self.p, self.far, 0)
        self.got_half(6, self.p, self.far, 1)
        self.put(7, self.p, self.far, self.pair_dev)
        self.share(self.p, self.far)

    def last_pair(self):
        for k, r in ((0, self.r), (3, self.prv), (4, self.nxt), (7, self.far)):
            self.got(k, self.q, r)
            self.share(self.q, r)

    def done(self, other_slot=None):
        for i, (p, r) in enumerate(self.shared):
            self.link.arrived(9 + i, other_slot(p, r), self.pair_dev)

    def sent(self):
        self.link.sent()


class Scatter:
    def __init__(self, link, parts, bufs, place, devs):
        self.link, self.parts = link, parts
        self.from_core, self.from_prev_half, self.from_next_half, self.from_prev, self.from_next, self.from_pair = bufs
        self.yl, self.z, self.c = place
        self.core_dev, self.pair_dev, self.next_dev, self.prev_dev = devs
        self.nxt, self.prv, self.far = (self.z + 1) % 4, (self.z + 3) % 4, (self.z + 2) % 4

    def give_core(self, ch):
        self.link.copy(
            ch, self.parts.at[ch, :, :, 1 - self.c], self.from_core.at[ch], self.core_dev
        ).start()

    def add_core(self):
        def step(ch, carry):
            self.link.copy(
                ch, self.parts.at[ch, :, :, 1 - self.c], self.from_core.at[ch], self.core_dev
            ).wait()
            own = self.parts[ch, :, :, self.c].astype(F32)
            self.parts[ch, :, :, self.c] = (own + self.from_core[ch].astype(F32)).astype(BF)
            return carry

        lax.fori_loop(0, CHUNKS, step, 0)

    def half(self, z, h):
        return self.parts.at[4 * h : 4 * h + 4, :, z, self.c]

    def start(self):
        link = self.link
        link.start(8, self.half(self.far, 0), self.from_prev_half, self.next_dev)
        link.start(9, self.half(self.far, 1), self.from_next_half, self.prev_dev)
        link.start(10, self.half(self.nxt, 1), self.from_prev.at[4:8], self.next_dev)
        link.start(11, self.half(self.prv, 0), self.from_next.at[0:4], self.prev_dev)

    def middle(self):
        link = self.link
        link.arrived(8, self.from_prev_half, self.pair_dev)
        for ch in range(4):
            mine = self.parts[ch, :, self.nxt, self.c].astype(F32)
            self.parts[ch, :, self.nxt, self.c] = (mine + self.from_prev_half[ch].astype(F32)).astype(BF)
        link.start(12, self.half(self.nxt, 0), self.from_prev.at[0:4], self.next_dev)
        link.arrived(9, self.from_next_half, self.pair_dev)
        for ch in range(4):
            mine = self.parts[4 + ch, :, self.prv, self.c].astype(F32)
            self.parts[4 + ch, :, self.prv, self.c] = (mine + self.from_next_half[ch].astype(F32)).astype(BF)
        link.start(13, self.half(self.prv, 1), self.from_next.at[4:8], self.prev_dev)

    def to_pair(self):
        link = self.link
        link.arrived(10, self.from_prev.at[4:8], self.pair_dev)
        link.arrived(11, self.from_next.at[0:4], self.pair_dev)
        for k, h in ((12, 0), (13, 1)):
            buf = self.from_prev if h == 0 else self.from_next
            link.arrived(k, buf.at[4 * h : 4 * h + 4], self.pair_dev)
            for ch in range(4 * h, 4 * h + 4):
                total = (
                    self.parts[ch, :, self.z, self.c].astype(F32)
                    + self.from_prev[ch].astype(F32)
                    + self.from_next[ch].astype(F32)
                )
                self.parts[ch, :, self.z, self.c] = total.astype(BF)
            link.start(
                14 + h,
                self.parts.at[4 * h : 4 * h + 4, 1 - self.yl, self.z, self.c],
                self.from_pair.at[4 * h : 4 * h + 4],
                self.pair_dev,
            )

    def arrived(self, h):
        self.link.arrived(14 + h, self.from_pair.at[4 * h : 4 * h + 4], self.pair_dev)

    def chunk(self, ch):
        return self.parts[ch, self.yl, self.z, self.c].astype(F32) + self.from_pair[ch].astype(F32)

    def sent(self):
        self.link.sent()


def layer(
    inputs_ref, gain_ref, doc_ref, wq_hbm, wk_hbm, wv_hbm, wo_hbm, gout_ref,
    out_ref, gin_ref, ggain_ref, gwq_ref, gwk_ref, gwv_ref, gwo_ref,
    xs, gs, nc, gc, pg, wq, wkv, wo, att, qkv, acc, kvh, kvg, qh, probs,
    rs0, rs1, rs2, rs3, rs4, rs5, rt1, rt2, rt3, rt4, rt5,
    ga0, ga1, ga2,
    x_s, x_r, g_s, g_r, nc_s, nc_r, gc_s, gc_r, at_s, at_r, qk_s, qk_r, ro_s, ro_r, rg_s, rg_r,
    tn_s, tn_r, kv_s, kv_r, ga_s, ga_r, w_sem,
):
    dp, head = lax.axis_index("dp"), lax.axis_index("head")
    x, yh = dp // 2, dp % 2
    yl, z, c = head // 8, (head // 2) % 4, head % 2
    core_dev = device(x, yh, yl, z, 1 - c)
    pair_dev = device(x, yh, 1 - yl, z, c)
    z_dev = [device(x, yh, yl, (z + k) % 4, c) for k in range(4)]
    dp_devs = [((dp + k) % 8, head) for k in range(1, 8)]
    x_dev = [device((x + k) % 4, yh, yl, z, c) for k in range(4)]
    yh_dev = device(x, 1 - yh, yl, z, c)
    diag_dev = device(x, yh, 1 - yl, z, 1 - c)

    weights = [
        pltpu.make_async_copy(wq_hbm, wq, w_sem.at[0]),
        pltpu.make_async_copy(wk_hbm, wkv.at[0 : HD // 2], w_sem.at[1]),
        pltpu.make_async_copy(wv_hbm, wkv.at[HD // 2 : HD], w_sem.at[2]),
        pltpu.make_async_copy(wo_hbm, wo, w_sem.at[3]),
    ]
    for cp in weights:
        cp.start()

    barrier = pltpu.get_barrier_semaphore()
    partners = [core_dev, pair_dev, diag_dev] + z_dev[1:] + dp_devs
    for to in partners:
        pl.semaphore_signal(barrier, inc=1, device_id=to, device_id_type=MESH)

    square = jnp.zeros((ROWS, 1), F32)
    for ch in range(CHUNKS):
        part = inputs_ref[:, ch * CHUNK : (ch + 1) * CHUNK].astype(F32)
        square += jnp.sum(part * part, axis=-1, keepdims=True)
    inverse_rms = lax.rsqrt(square * (1.0 / (CHUNKS * CHUNK)) + EPSILON)
    for ch in range(CHUNKS):
        cols = slice(ch * CHUNK, (ch + 1) * CHUNK)
        part = inputs_ref[:, cols].astype(F32)
        xs[ch, yl, z, c] = (part * inverse_rms * gain_ref[:, cols]).astype(BF)
        gs[ch, yl, z, c] = gout_ref[:, cols]
    nc[dp, yl, z, c] = xs[dp, yl, z, c]

    pl.semaphore_wait(barrier, len(partners))

    def head_gather(buf, send, recv):
        return Gather(
            Link(send, recv),
            lambda p, r: buf.at[:, p, r, c],
            lambda p, r, h: buf.at[4 * h : 4 * h + 4, p, r, c],
            (yl, z), pair_dev, (z_dev[1], z_dev[3]), core_dev,
        )

    def other_core(buf):
        return lambda p, r: buf.at[:, p, r, 1 - c]

    def dp_gather(buf, send, recv):
        return Gather(
            Link(send, recv),
            lambda p, r: buf.at[r, p],
            lambda p, r, h: buf.at[r, p, 128 * h : 128 * h + 128],
            (yh, x), yh_dev, (x_dev[1], x_dev[3]), None,
        )

    gx, gg = head_gather(xs, x_s, x_r), head_gather(gs, g_s, g_r)
    gnc = head_gather(nc, nc_s, nc_r)
    cols = Link(gc_s, gc_r)
    gat, gqk = dp_gather(att, at_s, at_r), dp_gather(qkv, qk_s, qk_r)
    devs = (core_dev, pair_dev, z_dev[1], z_dev[3])
    ro = Scatter(Link(ro_s, ro_r), xs, (rs0, rs1, rs2, rs3, rs4, rs5), (yl, z, c), devs)
    rg = Scatter(Link(rg_s, rg_r), pg, (rs0, rt1, rt2, rt3, rt4, rt5), (yl, z, c), devs)

    gx.start_ring()
    gx.start_pair()
    gg.start_pair()
    tiny = Link(tn_s, tn_r)
    for k in range(1, 8):
        to = (dp + k) % 8
        tiny.start(k - 1, xs.at[to, yl, z, c], nc.at[dp, yl, z, c], (to, head))

    row_index = lax.broadcasted_iota(jnp.int32, (SEQ, SEQ), 0)
    col_index = lax.broadcasted_iota(jnp.int32, (SEQ, SEQ), 1)
    doc_rows = jnp.broadcast_to(doc_ref[...].astype(F32), (SEQ, SEQ))
    same = doc_rows == doc_rows.T
    allowed = same & (col_index <= row_index)
    position = jnp.sum(jnp.where(allowed, 1.0, 0.0), axis=-1, keepdims=True) - 1.0
    lane = lax.broadcasted_iota(jnp.int32, (SEQ, HD), 1)
    low_half = lane < HD // 2
    exponent = jnp.where(low_half, lane, lane - HD // 2).astype(F32) * (2.0 / HD)
    angles = position * jnp.exp(exponent * -LOG_THETA)
    cosine, sine = jnp.cos(angles), jnp.sin(angles)
    sine_turn = jnp.where(low_half, -sine, sine)

    def rope(u):
        return u * cosine + pltpu.roll(u, HD // 2, 1) * sine_turn

    def rope_back(g):
        turned = pltpu.roll(g * sine, HD // 2, 1)
        return g * cosine + jnp.where(low_half, turned, -turned)

    gx.on_pair()
    gx.on_ring_own()
    gx.on_ring_pair()
    gg.start_ring()
    gg.on_pair()
    gx.on_far()
    gx.done(other_core(xs))

    for cp in weights[:3]:
        cp.wait()

    def project(ch, carry):
        block = xs[ch].reshape(SEQ, CHUNK)
        rows = pl.ds(pl.multiple_of(ch * CHUNK, CHUNK), CHUNK)
        acc[...] += dot(block, wq[rows, :])
        kvh_acc[...] += dot_nt(block, wkv[:, rows])
        return carry

    kvh_acc = probs.at[0, :, 0:HD]
    acc[...] = jnp.zeros_like(acc)
    kvh_acc[...] = jnp.zeros((SEQ, HD), F32)
    lax.fori_loop(0, CHUNKS, project, 0)
    kvh[c] = kvh_acc[...].astype(BF)
    kv_link = Link(kv_s, kv_r)
    kv_link.start(0, kvh.at[c], kvh.at[c], core_dev)
    gg.on_ring_own()
    for h in range(HEADS):
        pre = acc[:, h * HD : (h + 1) * HD].astype(BF).astype(F32)
        qh[h] = rope(pre).astype(BF)
    kv_link.arrived(0, kvh.at[1 - c], core_dev)
    first, second = kvh[0].astype(F32), kvh[1].astype(F32)
    key_pre = jnp.where(low_half, first, pltpu.roll(second, HD // 2, 1))
    values = jnp.where(low_half, pltpu.roll(first, HD // 2, 1), second).astype(BF)
    key_rows = rope(key_pre).astype(BF)
    score_scale = HD ** (-0.5)

    for h in range(HEADS):
        scores = dot_nt(qh[h], key_rows) * score_scale
        scores = jnp.where(allowed, scores, -1e30)
        top = jnp.max(scores, axis=-1, keepdims=True)
        e = jnp.exp(scores - top)
        p = e / jnp.sum(e, axis=-1, keepdims=True)
        probs[h] = p
        att[x, yh, :, h * HD : (h + 1) * HD] = dot(p.astype(BF), values).astype(BF)
    gat.start_ring()
    gat.start_pair()
    gg.on_ring_pair()

    gx.sent()
    tiny.sent()
    weights[3].wait()
    wide = (2, 4, 2, ROWS, CHUNK)

    def project_out(ch, carry):
        cols_ch = pl.ds(pl.multiple_of(ch * CHUNK, CHUNK), CHUNK)
        xs[ch] = dot(att[x, yh], wo[:, cols_ch]).astype(BF).reshape(wide)
        ro.give_core(ch)
        return carry

    lax.fori_loop(0, CHUNKS, project_out, 0)
    ro.add_core()
    gg.on_far()
    ro.start()
    gat.on_pair()
    gg.done(other_core(gs))

    for k in range(1, 8):
        to = (dp + k) % 8
        cols.start(k - 1, gs.at[to, :, :, c], gc.at[dp, :, :, c], (to, head))
    gc[dp] = gs[dp]
    for k in range(1, 8):
        tiny.arrived(k - 1, nc.at[(dp + 8 - k) % 8, yl, z, c], core_dev)
    gnc.start_pair()

    acc[...] = jnp.zeros_like(acc)

    def back_out(ch, carry):
        cols_ch = pl.ds(pl.multiple_of(ch * CHUNK, CHUNK), CHUNK)
        acc[...] += dot_nt(gs[ch].reshape(SEQ, CHUNK), wo[:, cols_ch])
        return carry

    lax.fori_loop(0, CHUNKS, back_out, 0)
    gat.on_ring_own()
    key_sum = jnp.zeros((SEQ, HD), F32)
    value_sum = jnp.zeros((SEQ, HD), F32)
    for h in range(HEADS):
        grad_att = acc[:, h * HD : (h + 1) * HD].astype(BF)
        p = probs[h]
        grad_probs = dot_nt(grad_att, values)
        delta = jnp.sum(p * grad_probs, axis=-1, keepdims=True)
        grad_scores = (p * (grad_probs - delta)).astype(BF)
        grad_query = dot(grad_scores, key_rows) * score_scale
        qkv[x, yh, :, h * HD : (h + 1) * HD] = rope_back(grad_query).astype(BF)
        key_sum += dot_tn(grad_scores, qh[h])
        value_sum += dot_tn(p.astype(BF), grad_att)
    kvg[c, 0] = rope_back(key_sum * score_scale).astype(BF)
    kvg[c, 1] = value_sum.astype(BF)
    kv_link.start(1, kvg.at[c], kvg.at[c], core_dev)
    ro.middle()
    kv_link.arrived(1, kvg.at[1 - c], core_dev)
    key_pair = (kvg[0, 0].astype(F32) + kvg[1, 0].astype(F32)).astype(BF).astype(F32)
    value_pair = (kvg[0, 1].astype(F32) + kvg[1, 1].astype(F32)).astype(BF).astype(F32)
    even = jnp.where(low_half, key_pair, pltpu.roll(value_pair, HD // 2, 1))
    odd = jnp.where(low_half, pltpu.roll(key_pair, HD // 2, 1), value_pair)
    qkv[x, yh, :, HEADS * HD :] = jnp.where(c == 0, even, odd).astype(BF)
    gqk.start_ring()
    gqk.start_pair()
    gat.on_ring_pair()

    def back_in(ch, carry):
        rows = pl.ds(pl.multiple_of(ch * CHUNK, CHUNK), CHUNK)
        part = dot_nt(qkv[x, yh, :, : HEADS * HD], wq[rows, :])
        part += dot(qkv[x, yh, :, HEADS * HD :], wkv[:, rows])
        pg[ch] = part.astype(BF).reshape(wide)
        rg.give_core(ch)
        return carry

    lax.fori_loop(0, CHUNKS, back_in, 0)
    rg.add_core()
    rg.start()
    gnc.start_ring()
    gqk.on_pair()
    ro.to_pair()
    gat.on_far()
    gqk.on_ring_own()
    rg.middle()
    for h in range(2):
        ro.arrived(h)
        for ch in range(4 * h, 4 * h + 4):
            span = slice(ch * CHUNK, (ch + 1) * CHUNK)
            out_ref[:, span] = (inputs_ref[:, span].astype(F32) + ro.chunk(ch)).astype(BF)
    gqk.on_ring_pair()
    gnc.last_ring()
    for k in range(1, 8):
        block = gc.at[(dp + 8 - k) % 8, :, :, c]
        cols.arrived(k - 1, block, core_dev)
        cols.start(6 + k, block, block, core_dev)
    rg.to_pair()
    gnc.last_far()

    mean = jnp.zeros((ROWS, 1), F32)
    gain_slot = yl * 2 + c
    for h in range(2):
        rg.arrived(h)
        for ch in range(4 * h, 4 * h + 4):
            span = slice(ch * CHUNK, (ch + 1) * CHUNK)
            grad = rg.chunk(ch)
            part = inputs_ref[:, span].astype(F32)
            ga0[gain_slot, ch : ch + 1] = jnp.sum(grad * part * inverse_rms, axis=0, keepdims=True)
            mean += jnp.sum(grad * gain_ref[:, span] * part, axis=-1, keepdims=True)
    ga_link = Link(ga_s, ga_r)
    near = [(core_dev, yl * 2 + 1 - c), (pair_dev, (1 - yl) * 2 + c), (diag_dev, (1 - yl) * 2 + 1 - c)]
    for k, (to, _) in enumerate(near):
        ga_link.start(k, ga0.at[gain_slot], ga0.at[gain_slot], to)
    mean = mean * (1.0 / (CHUNKS * CHUNK)) * inverse_rms * inverse_rms * inverse_rms
    for ch in range(CHUNKS):
        span = slice(ch * CHUNK, (ch + 1) * CHUNK)
        part = inputs_ref[:, span].astype(F32)
        scaled = rg.chunk(ch) * gain_ref[:, span]
        gin_ref[:, span] = (gout_ref[:, span].astype(F32) + inverse_rms * scaled - part * mean).astype(BF)
    for k, (_, slot) in enumerate(near):
        ga_link.arrived(k, ga0.at[slot], core_dev)
    ga1[z] = (ga0[0] + ga0[1]) + (ga0[2] + ga0[3])
    for k in range(1, 4):
        ga_link.start(2 + k, ga1.at[z], ga1.at[z], z_dev[k])

    gnc.last_pair()
    for k in range(1, 4):
        ga_link.arrived(2 + k, ga1.at[(z + 4 - k) % 4], core_dev)
    ga2[dp] = (ga1[0] + ga1[1]) + (ga1[2] + ga1[3])
    for k in range(1, 8):
        ga_link.start(5 + k, ga2.at[dp], ga2.at[dp], ((dp + k) % 8, head))

    for k in range(1, 8):
        cols.arrived(6 + k, gc.at[(dp + 8 - k) % 8, :, :, 1 - c], core_dev)
    total = None
    for s in range(8):
        term = dot_tn(att[s // 2, s % 2], gc[s].reshape(SEQ, CHUNK))
        total = term if total is None else total + term
    gwo_ref[...] = total.astype(BF)
    gqk.on_far()
    gnc.done(other_core(nc))
    total = None
    for s in range(8):
        term = dot_tn(nc[s].reshape(SEQ, CHUNK), qkv[s // 2, s % 2])
        total = term if total is None else total + term
    gwq_ref[...] = total[:, : HEADS * HD].astype(BF)
    pairs = total[:, HEADS * HD :].T
    gwk_ref[...] = pairs[: HD // 2].astype(BF)
    gwv_ref[...] = pairs[HD // 2 :].astype(BF)

    for k in range(1, 8):
        ga_link.arrived(5 + k, ga2.at[(dp + 8 - k) % 8], core_dev)
    total = ((ga2[0] + ga2[1]) + (ga2[2] + ga2[3])) + ((ga2[4] + ga2[5]) + (ga2[6] + ga2[7]))
    for ch in range(CHUNKS):
        ggain_ref[:, ch * CHUNK : (ch + 1) * CHUNK] = total[ch : ch + 1]

    for link in (gg, gat, gqk, gnc, cols, ro, rg, kv_link, ga_link):
        link.sent()


def hand_over(*refs):
    src, dst, mid, sem_in, sem_out = refs[:7], refs[7:14], refs[14:21], refs[21], refs[22]
    loads = [pltpu.make_async_copy(src[i], mid[i], sem_in.at[i]) for i in range(7)]
    stores = [pltpu.make_async_copy(mid[i], dst[i], sem_out.at[i]) for i in range(7)]
    for cp in loads:
        cp.start()
    for load, store in zip(loads, stores):
        load.wait()
        store.start()
    for cp in stores:
        cp.wait()


def per_device(inputs, gain, doc_ids, w_query, w_key, w_value, w_out, grad_out):
    vmem = pl.BlockSpec(memory_space=pltpu.VMEM)
    hbm = pl.BlockSpec(memory_space=pl.ANY)
    rows = (CHUNKS, 2, 4, 2, ROWS, CHUNK)
    half = (4, 2, ROWS, CHUNK)
    scatter = [
        pltpu.VMEM((CHUNKS, 2, 4, ROWS, CHUNK), BF),
        pltpu.VMEM(half, BF),
        pltpu.VMEM(half, BF),
        pltpu.VMEM((CHUNKS, 2, ROWS, CHUNK), BF),
        pltpu.VMEM((CHUNKS, 2, ROWS, CHUNK), BF),
        pltpu.VMEM((CHUNKS, ROWS, CHUNK), BF),
    ]
    dma = lambda n: [pltpu.SemaphoreType.DMA((n,))] * 2
    outs = pl.pallas_call(
        layer,
        out_shape=(
            jax.ShapeDtypeStruct((ROWS, CHUNKS * CHUNK), BF),
            jax.ShapeDtypeStruct((ROWS, CHUNKS * CHUNK), BF),
            jax.ShapeDtypeStruct((1, CHUNKS * CHUNK), F32),
            jax.ShapeDtypeStruct((CHUNK, HEADS * HD), BF),
            jax.ShapeDtypeStruct((HD // 2, CHUNK), BF),
            jax.ShapeDtypeStruct((HD // 2, CHUNK), BF),
            jax.ShapeDtypeStruct((HEADS * HD, CHUNK), BF),
        ),
        in_specs=[vmem] * 3 + [hbm] * 4 + [vmem],
        out_specs=[vmem] * 7,
        scratch_shapes=[
            pltpu.VMEM(rows, BF),
            pltpu.VMEM(rows, BF),
            pltpu.VMEM(rows, BF),
            pltpu.VMEM(rows, BF),
            pltpu.VMEM(rows, BF),
            pltpu.VMEM((CHUNKS * CHUNK, HEADS * HD), BF),
            pltpu.VMEM((HD, CHUNKS * CHUNK), BF),
            pltpu.VMEM((HEADS * HD, CHUNKS * CHUNK), BF),
            pltpu.VMEM((4, 2, SEQ, HEADS * HD), BF),
            pltpu.VMEM((4, 2, SEQ, HEADS * HD + HD), BF),
            pltpu.VMEM((SEQ, HEADS * HD), F32),
            pltpu.VMEM((2, SEQ, HD), BF),
            pltpu.VMEM((2, 2, SEQ, HD), BF),
            pltpu.VMEM((HEADS, SEQ, HD), BF),
            pltpu.VMEM((HEADS, SEQ, SEQ), F32),
        ]
        + scatter
        + scatter[1:]
        + [
            pltpu.VMEM((4, CHUNKS, CHUNK), F32),
            pltpu.VMEM((4, CHUNKS, CHUNK), F32),
            pltpu.VMEM((8, CHUNKS, CHUNK), F32),
        ]
        + dma(17) * 4
        + dma(9) * 2
        + dma(16) * 2
        + dma(7)
        + dma(2)
        + dma(13)
        + [pltpu.SemaphoreType.DMA((4,))],
        compiler_params=pltpu.CompilerParams(
            collective_id=0, has_side_effects=True, vmem_limit_bytes=60 * 2**20
        ),
    )(
        inputs,
        gain[None, :],
        doc_ids,
        w_query,
        w_key.T,
        w_value.T,
        w_out,
        grad_out,
    )
    out, gin, ggain, gwq, gwk, gwv, gwo = pl.pallas_call(
        hand_over,
        out_shape=[jax.ShapeDtypeStruct(o.shape, o.dtype) for o in outs],
        in_specs=[hbm] * 7,
        out_specs=[hbm] * 7,
        scratch_shapes=[pltpu.VMEM(o.shape, o.dtype) for o in outs] + dma(7),
    )(*outs)
    return (out, gin, ggain.reshape(-1), gwq, gwk.T, gwv.T, gwo)


def solution(mesh):
    return jax.shard_map(
        per_device,
        mesh=mesh,
        in_specs=(
            P(("dp", "head"), None),
            P(),
            P("dp", None),
            P(None, "head"),
            P(None, "head"),
            P(None, "head"),
            P("head", None),
            P(("dp", "head"), None),
        ),
        out_specs=(
            P(("dp", "head"), None),
            P(("dp", "head"), None),
            P(),
            P("dp", "head"),
            P("dp", "head"),
            P("dp", "head"),
            P("head", "dp"),
        ),
        check_vma=False,
    )
```

```python
import math

import jax
import jax.numpy as jnp
from jax import lax
from jax.experimental import pallas as pl
from jax.experimental.pallas import tpu as pltpu
from jax.sharding import PartitionSpec as P

EPSILON = 1e-05
LOG_THETA = math.log(500000.0)
MESH = pl.DeviceIdType.MESH
BF = jnp.bfloat16
F32 = jnp.float32

ROWS = 16
CHUNKS = 8
CHUNK = 1024
SEQ = 256
HEADS = 4
HD = 128


def device(x, yh, yl, z, c):
    return (x * 2 + yh, (yl * 4 + z) * 2 + c)


def dot(a, b):
    return jnp.dot(a, b, preferred_element_type=F32)


def dot_nt(a, b):
    return lax.dot_general(a, b, (((1,), (1,)), ((), ())), preferred_element_type=F32)


def dot_tn(a, b):
    return lax.dot_general(a, b, (((0,), (0,)), ((), ())), preferred_element_type=F32)


class Link:
    def __init__(self, send, recv):
        self.send, self.recv, self.started = send, recv, []

    def copy(self, k, src, dst, to):
        return pltpu.make_async_remote_copy(
            src_ref=src,
            dst_ref=dst,
            send_sem=self.send.at[k],
            recv_sem=self.recv.at[k],
            device_id=to,
            device_id_type=MESH,
        )

    def start(self, k, src, dst, to):
        cp = self.copy(k, src, dst, to)
        cp.start()
        self.started.append(cp)

    def arrived(self, k, dst, to):
        self.copy(k, dst, dst, to).wait_recv()

    def sent(self):
        for cp in self.started:
            cp.wait_send()
        self.started = []


class Gather:
    def __init__(self, link, slot, half, place, pair, ring, core):
        self.link, self.slot, self.half = link, slot, half
        self.p, self.r = place
        self.pair_dev, self.core_dev = pair, core
        self.next_dev, self.prev_dev = ring
        self.q = 1 - self.p
        self.nxt, self.prv, self.far = (self.r + 1) % 4, (self.r + 3) % 4, (self.r + 2) % 4
        self.shared = []

    def put(self, k, p, r, to):
        ref = self.slot(p, r)
        self.link.start(k, ref, ref, to)

    def put_half(self, k, p, r, h, to):
        ref = self.half(p, r, h)
        self.link.start(k, ref, ref, to)

    def got(self, k, p, r):
        self.link.arrived(k, self.slot(p, r), self.pair_dev)

    def got_half(self, k, p, r, h):
        self.link.arrived(k, self.half(p, r, h), self.pair_dev)

    def share(self, p, r):
        if self.core_dev is not None:
            self.put(9 + len(self.shared), p, r, self.core_dev)
            self.shared.append((p, r))

    def start_pair(self):
        self.put(0, self.p, self.r, self.pair_dev)

    def start_ring(self):
        self.put(1, self.p, self.r, self.next_dev)
        self.put(2, self.p, self.r, self.prev_dev)
        self.share(self.p, self.r)

    def on_pair(self):
        self.got(0, self.q, self.r)
        self.put(3, self.q, self.r, self.next_dev)
        self.put(4, self.q, self.r, self.prev_dev)
        self.share(self.q, self.r)

    def on_ring(self, p, base, k):
        self.got(base, p, self.prv)
        self.put_half(k, p, self.prv, 0, self.next_dev)
        self.share(p, self.prv)
        self.got(base + 1, p, self.nxt)
        self.put_half(k + 1, p, self.nxt, 1, self.prev_dev)
        self.share(p, self.nxt)

    def on_ring_own(self):
        self.on_ring(self.p, 1, 5)

    def on_ring_pair(self):
        self.on_ring(self.q, 3, 7)

    def on_far(self):
        for p, k in ((self.p, 5), (self.q, 7)):
            self.got_half(k, p, self.far, 0)
            self.got_half(k + 1, p, self.far, 1)
            self.share(p, self.far)

    def last_ring(self):
        self.got(1, self.p, self.prv)
        self.put_half(5, self.p, self.prv, 0, self.next_dev)
        self.put(3, self.p, self.prv, self.pair_dev)
        self.share(self.p, self.prv)
        self.got(2, self.p, self.nxt)
        self.put_half(6, self.p, self.nxt, 1, self.prev_dev)
        self.put(4, self.p, self.nxt, self.pair_dev)
        self.share(self.p, self.nxt)

    def last_far(self):
        self.got_half(5, self.p, self.far, 0)
        self.got_half(6, self.p, self.far, 1)
        self.put(7, self.p, self.far, self.pair_dev)
        self.share(self.p, self.far)

    def last_pair(self):
        for k, r in ((0, self.r), (3, self.prv), (4, self.nxt), (7, self.far)):
            self.got(k, self.q, r)
            self.share(self.q, r)

    def done(self, other_slot=None):
        for i, (p, r) in enumerate(self.shared):
            self.link.arrived(9 + i, other_slot(p, r), self.pair_dev)

    def sent(self):
        self.link.sent()


class Scatter:
    def __init__(self, link, parts, bufs, place, devs):
        self.link, self.parts = link, parts
        self.from_core, self.from_prev_half, self.from_next_half, self.from_prev, self.from_next, self.from_pair = bufs
        self.yl, self.z, self.c = place
        self.core_dev, self.pair_dev, self.next_dev, self.prev_dev = devs
        self.nxt, self.prv, self.far = (self.z + 1) % 4, (self.z + 3) % 4, (self.z + 2) % 4

    def give_core(self, ch):
        self.link.copy(
            ch, self.parts.at[ch, :, :, 1 - self.c], self.from_core.at[ch], self.core_dev
        ).start()

    def add_core(self):
        def step(ch, carry):
            self.link.copy(
                ch, self.parts.at[ch, :, :, 1 - self.c], self.from_core.at[ch], self.core_dev
            ).wait()
            own = self.parts[ch, :, :, self.c].astype(F32)
            self.parts[ch, :, :, self.c] = (own + self.from_core[ch].astype(F32)).astype(BF)
            return carry

        lax.fori_loop(0, CHUNKS, step, 0)

    def half(self, z, h):
        return self.parts.at[4 * h : 4 * h + 4, :, z, self.c]

    def start(self):
        link = self.link
        link.start(8, self.half(self.far, 0), self.from_prev_half, self.next_dev)
        link.start(9, self.half(self.far, 1), self.from_next_half, self.prev_dev)
        link.start(10, self.half(self.nxt, 1), self.from_prev.at[4:8], self.next_dev)
        link.start(11, self.half(self.prv, 0), self.from_next.at[0:4], self.prev_dev)

    def middle(self):
        link = self.link
        link.arrived(8, self.from_prev_half, self.pair_dev)
        for ch in range(4):
            mine = self.parts[ch, :, self.nxt, self.c].astype(F32)
            self.parts[ch, :, self.nxt, self.c] = (mine + self.from_prev_half[ch].astype(F32)).astype(BF)
        link.start(12, self.half(self.nxt, 0), self.from_prev.at[0:4], self.next_dev)
        link.arrived(9, self.from_next_half, self.pair_dev)
        for ch in range(4):
            mine = self.parts[4 + ch, :, self.prv, self.c].astype(F32)
            self.parts[4 + ch, :, self.prv, self.c] = (mine + self.from_next_half[ch].astype(F32)).astype(BF)
        link.start(13, self.half(self.prv, 1), self.from_next.at[4:8], self.prev_dev)

    def to_pair(self):
        link = self.link
        link.arrived(10, self.from_prev.at[4:8], self.pair_dev)
        link.arrived(11, self.from_next.at[0:4], self.pair_dev)
        for k, h in ((12, 0), (13, 1)):
            buf = self.from_prev if h == 0 else self.from_next
            link.arrived(k, buf.at[4 * h : 4 * h + 4], self.pair_dev)
            for ch in range(4 * h, 4 * h + 4):
                total = (
                    self.parts[ch, :, self.z, self.c].astype(F32)
                    + self.from_prev[ch].astype(F32)
                    + self.from_next[ch].astype(F32)
                )
                self.parts[ch, :, self.z, self.c] = total.astype(BF)
            link.start(
                14 + h,
                self.parts.at[4 * h : 4 * h + 4, 1 - self.yl, self.z, self.c],
                self.from_pair.at[4 * h : 4 * h + 4],
                self.pair_dev,
            )

    def arrived(self, h):
        self.link.arrived(14 + h, self.from_pair.at[4 * h : 4 * h + 4], self.pair_dev)

    def chunk(self, ch):
        return self.parts[ch, self.yl, self.z, self.c].astype(F32) + self.from_pair[ch].astype(F32)

    def sent(self):
        self.link.sent()


def layer(
    inputs_ref, gain_ref, doc_ref, wq_hbm, wk_hbm, wv_hbm, wo_hbm, gout_ref,
    out_ref, gin_ref, ggain_ref, gwq_ref, gwk_ref, gwv_ref, gwo_ref,
    xs, gs, nc, gc, po, wq, wkv, wo, att, qkv, acc, kvh, kvg, qh, probs,
    rs0, rs1, rs2, rs3, rs4, rs5, rt1, rt2, rt3, rt4, rt5,
    ga0, ga1, ga2,
    x_s, x_r, g_s, g_r, nc_s, nc_r, gc_s, gc_r, at_s, at_r, qk_s, qk_r, ro_s, ro_r, rg_s, rg_r,
    tn_s, tn_r, kv_s, kv_r, ga_s, ga_r, w_sem,
):
    dp, head = lax.axis_index("dp"), lax.axis_index("head")
    x, yh = dp // 2, dp % 2
    yl, z, c = head // 8, (head // 2) % 4, head % 2
    core_dev = device(x, yh, yl, z, 1 - c)
    pair_dev = device(x, yh, 1 - yl, z, c)
    z_dev = [device(x, yh, yl, (z + k) % 4, c) for k in range(4)]
    dp_devs = [((dp + k) % 8, head) for k in range(1, 8)]
    x_dev = [device((x + k) % 4, yh, yl, z, c) for k in range(4)]
    yh_dev = device(x, 1 - yh, yl, z, c)
    diag_dev = device(x, yh, 1 - yl, z, 1 - c)

    weights = [
        pltpu.make_async_copy(wq_hbm, wq, w_sem.at[0]),
        pltpu.make_async_copy(wk_hbm, wkv.at[0 : HD // 2], w_sem.at[1]),
        pltpu.make_async_copy(wv_hbm, wkv.at[HD // 2 : HD], w_sem.at[2]),
        pltpu.make_async_copy(wo_hbm, wo, w_sem.at[3]),
    ]
    for cp in weights:
        cp.start()

    barrier = pltpu.get_barrier_semaphore()
    partners = [core_dev, pair_dev, diag_dev] + z_dev[1:] + dp_devs
    for to in partners:
        pl.semaphore_signal(barrier, inc=1, device_id=to, device_id_type=MESH)

    square = jnp.zeros((ROWS, 1), F32)
    for ch in range(CHUNKS):
        part = inputs_ref[:, ch * CHUNK : (ch + 1) * CHUNK].astype(F32)
        square += jnp.sum(part * part, axis=-1, keepdims=True)
    inverse_rms = lax.rsqrt(square * (1.0 / (CHUNKS * CHUNK)) + EPSILON)
    for ch in range(CHUNKS):
        cols = slice(ch * CHUNK, (ch + 1) * CHUNK)
        part = inputs_ref[:, cols].astype(F32)
        xs[ch, yl, z, c] = (part * inverse_rms * gain_ref[:, cols]).astype(BF)
        gs[ch, yl, z, c] = gout_ref[:, cols]
    gc[dp, yl, z, c] = gs[dp, yl, z, c]

    pl.semaphore_wait(barrier, len(partners))

    def head_gather(buf, send, recv):
        return Gather(
            Link(send, recv),
            lambda p, r: buf.at[:, p, r, c],
            lambda p, r, h: buf.at[4 * h : 4 * h + 4, p, r, c],
            (yl, z), pair_dev, (z_dev[1], z_dev[3]), core_dev,
        )

    def other_core(buf):
        return lambda p, r: buf.at[:, p, r, 1 - c]

    def dp_gather(buf, send, recv):
        return Gather(
            Link(send, recv),
            lambda p, r: buf.at[r, p],
            lambda p, r, h: buf.at[r, p, 128 * h : 128 * h + 128],
            (yh, x), yh_dev, (x_dev[1], x_dev[3]), None,
        )

    gx, gg = head_gather(xs, x_s, x_r), head_gather(gs, g_s, g_r)
    ggc = head_gather(gc, gc_s, gc_r)
    cols = Link(nc_s, nc_r)
    gat, gqk = dp_gather(att, at_s, at_r), dp_gather(qkv, qk_s, qk_r)
    devs = (core_dev, pair_dev, z_dev[1], z_dev[3])
    ro = Scatter(Link(ro_s, ro_r), po, (rs0, rs1, rs2, rs3, rs4, rs5), (yl, z, c), devs)
    rg = Scatter(Link(rg_s, rg_r), gs, (rs0, rt1, rt2, rt3, rt4, rt5), (yl, z, c), devs)

    gx.start_ring()
    gx.start_pair()
    tiny = Link(tn_s, tn_r)
    for k in range(1, 8):
        to = (dp + k) % 8
        tiny.start(k - 1, gs.at[to, yl, z, c], gc.at[dp, yl, z, c], (to, head))

    row_index = lax.broadcasted_iota(jnp.int32, (SEQ, SEQ), 0)
    col_index = lax.broadcasted_iota(jnp.int32, (SEQ, SEQ), 1)
    doc_rows = jnp.broadcast_to(doc_ref[...].astype(F32), (SEQ, SEQ))
    same = doc_rows == doc_rows.T
    allowed = same & (col_index <= row_index)
    position = jnp.sum(jnp.where(allowed, 1.0, 0.0), axis=-1, keepdims=True) - 1.0
    lane = lax.broadcasted_iota(jnp.int32, (SEQ, HD), 1)
    low_half = lane < HD // 2
    exponent = jnp.where(low_half, lane, lane - HD // 2).astype(F32) * (2.0 / HD)
    angles = position * jnp.exp(exponent * -LOG_THETA)
    cosine, sine = jnp.cos(angles), jnp.sin(angles)
    sine_turn = jnp.where(low_half, -sine, sine)

    def rope(u):
        return u * cosine + pltpu.roll(u, HD // 2, 1) * sine_turn

    def rope_back(g):
        turned = pltpu.roll(g * sine, HD // 2, 1)
        return g * cosine + jnp.where(low_half, turned, -turned)

    gx.on_pair()
    gg.start_pair()
    gx.on_ring_own()
    gx.on_ring_pair()
    gg.start_ring()
    gg.on_pair()
    gx.on_far()
    gx.done(other_core(xs))

    for k in range(1, 8):
        to = (dp + k) % 8
        cols.start(k - 1, xs.at[to, :, :, c], nc.at[dp, :, :, c], (to, head))
    nc[dp] = xs[dp]

    for cp in weights[:3]:
        cp.wait()

    def project(ch, carry):
        block = xs[ch].reshape(SEQ, CHUNK)
        rows = pl.ds(pl.multiple_of(ch * CHUNK, CHUNK), CHUNK)
        acc[...] += dot(block, wq[rows, :])
        kvh_acc[...] += dot_nt(block, wkv[:, rows])
        return carry

    kvh_acc = probs.at[0, :, 0:HD]
    acc[...] = jnp.zeros_like(acc)
    kvh_acc[...] = jnp.zeros((SEQ, HD), F32)
    lax.fori_loop(0, CHUNKS, project, 0)
    kvh[c] = kvh_acc[...].astype(BF)
    kv_link = Link(kv_s, kv_r)
    kv_link.start(0, kvh.at[c], kvh.at[c], core_dev)
    gg.on_ring_own()
    for h in range(HEADS):
        pre = acc[:, h * HD : (h + 1) * HD].astype(BF).astype(F32)
        qh[h] = rope(pre).astype(BF)
    kv_link.arrived(0, kvh.at[1 - c], core_dev)
    first, second = kvh[0].astype(F32), kvh[1].astype(F32)
    key_pre = jnp.where(low_half, first, pltpu.roll(second, HD // 2, 1))
    values = jnp.where(low_half, pltpu.roll(first, HD // 2, 1), second).astype(BF)
    key_rows = rope(key_pre).astype(BF)
    score_scale = HD ** (-0.5)

    for h in range(HEADS):
        scores = dot_nt(qh[h], key_rows) * score_scale
        scores = jnp.where(allowed, scores, -1e30)
        top = jnp.max(scores, axis=-1, keepdims=True)
        e = jnp.exp(scores - top)
        p = e / jnp.sum(e, axis=-1, keepdims=True)
        probs[h] = p
        att[x, yh, :, h * HD : (h + 1) * HD] = dot(p.astype(BF), values).astype(BF)
    gat.start_ring()
    gat.start_pair()
    gg.on_ring_pair()

    weights[3].wait()
    wide = (2, 4, 2, ROWS, CHUNK)

    def project_out(ch, carry):
        cols_ch = pl.ds(pl.multiple_of(ch * CHUNK, CHUNK), CHUNK)
        po[ch] = dot(att[x, yh], wo[:, cols_ch]).astype(BF).reshape(wide)
        ro.give_core(ch)
        return carry

    lax.fori_loop(0, CHUNKS, project_out, 0)
    ro.add_core()
    gg.on_far()
    for k in range(1, 8):
        tiny.arrived(k - 1, gc.at[(dp + 8 - k) % 8, yl, z, c], core_dev)
    ggc.start_ring()
    ggc.start_pair()
    ro.start()
    gat.on_pair()
    gg.done(other_core(gs))

    acc[...] = jnp.zeros_like(acc)

    def back_out(ch, carry):
        cols_ch = pl.ds(pl.multiple_of(ch * CHUNK, CHUNK), CHUNK)
        acc[...] += dot_nt(gs[ch].reshape(SEQ, CHUNK), wo[:, cols_ch])
        return carry

    lax.fori_loop(0, CHUNKS, back_out, 0)
    gat.on_ring_own()
    ggc.on_pair()
    key_sum = jnp.zeros((SEQ, HD), F32)
    value_sum = jnp.zeros((SEQ, HD), F32)
    for h in range(HEADS):
        grad_att = acc[:, h * HD : (h + 1) * HD].astype(BF)
        p = probs[h]
        grad_probs = dot_nt(grad_att, values)
        delta = jnp.sum(p * grad_probs, axis=-1, keepdims=True)
        grad_scores = (p * (grad_probs - delta)).astype(BF)
        grad_query = dot(grad_scores, key_rows) * score_scale
        qkv[x, yh, :, h * HD : (h + 1) * HD] = rope_back(grad_query).astype(BF)
        key_sum += dot_tn(grad_scores, qh[h])
        value_sum += dot_tn(p.astype(BF), grad_att)
    kvg[c, 0] = rope_back(key_sum * score_scale).astype(BF)
    kvg[c, 1] = value_sum.astype(BF)
    kv_link.start(1, kvg.at[c], kvg.at[c], core_dev)
    ro.middle()
    kv_link.arrived(1, kvg.at[1 - c], core_dev)
    key_pair = (kvg[0, 0].astype(F32) + kvg[1, 0].astype(F32)).astype(BF).astype(F32)
    value_pair = (kvg[0, 1].astype(F32) + kvg[1, 1].astype(F32)).astype(BF).astype(F32)
    even = jnp.where(low_half, key_pair, pltpu.roll(value_pair, HD // 2, 1))
    odd = jnp.where(low_half, pltpu.roll(key_pair, HD // 2, 1), value_pair)
    qkv[x, yh, :, HEADS * HD :] = jnp.where(c == 0, even, odd).astype(BF)
    gqk.start_ring()
    gqk.start_pair()
    gat.on_ring_pair()
    ggc.on_ring_own()
    gg.sent()
    tiny.sent()

    def back_in(ch, carry):
        rows = pl.ds(pl.multiple_of(ch * CHUNK, CHUNK), CHUNK)
        part = dot_nt(qkv[x, yh, :, : HEADS * HD], wq[rows, :])
        part += dot(qkv[x, yh, :, HEADS * HD :], wkv[:, rows])
        gs[ch] = part.astype(BF).reshape(wide)
        rg.give_core(ch)
        return carry

    lax.fori_loop(0, CHUNKS, back_in, 0)
    rg.add_core()
    rg.start()

    gain_slot = yl * 2 + c
    for ch in range(CHUNKS):
        term = gs[ch, :, :, c].astype(F32) * xs[ch, :, :, c].astype(F32)
        term = jnp.sum(term.reshape(SEQ // 2, CHUNK), axis=0, keepdims=True)
        ga0[gain_slot, ch : ch + 1] = term / gain_ref[:, ch * CHUNK : (ch + 1) * CHUNK]
    ga_link = Link(ga_s, ga_r)
    near = [(core_dev, yl * 2 + 1 - c), (pair_dev, (1 - yl) * 2 + c), (diag_dev, (1 - yl) * 2 + 1 - c)]
    for k, (to, _) in enumerate(near):
        ga_link.start(k, ga0.at[gain_slot], ga0.at[gain_slot], to)

    gqk.on_pair()
    ro.to_pair()
    for k in range(1, 8):
        block = nc.at[(dp + 8 - k) % 8, :, :, c]
        cols.arrived(k - 1, block, core_dev)
        cols.start(6 + k, block, block, core_dev)
    for k, (_, slot) in enumerate(near):
        ga_link.arrived(k, ga0.at[slot], core_dev)
    ga1[z] = (ga0[0] + ga0[1]) + (ga0[2] + ga0[3])
    for k in range(1, 4):
        ga_link.start(2 + k, ga1.at[z], ga1.at[z], z_dev[k])
    gat.on_far()
    gqk.on_ring_own()
    rg.middle()
    ggc.on_ring_pair()
    for h in range(2):
        ro.arrived(h)
        for ch in range(4 * h, 4 * h + 4):
            span = slice(ch * CHUNK, (ch + 1) * CHUNK)
            out_ref[:, span] = (inputs_ref[:, span].astype(F32) + ro.chunk(ch)).astype(BF)
    gqk.on_ring_pair()
    for k in range(1, 4):
        ga_link.arrived(2 + k, ga1.at[(z + 4 - k) % 4], core_dev)
    ga2[dp] = (ga1[0] + ga1[1]) + (ga1[2] + ga1[3])
    for k in range(1, 8):
        ga_link.start(5 + k, ga2.at[dp], ga2.at[dp], ((dp + k) % 8, head))
    for k in range(1, 8):
        cols.arrived(6 + k, nc.at[(dp + 8 - k) % 8, :, :, 1 - c], core_dev)

    gqk.on_far()
    total = None
    for s in range(8):
        term = dot_tn(nc[s].reshape(SEQ, CHUNK), qkv[s // 2, s % 2])
        total = term if total is None else total + term
    gwq_ref[...] = total[:, : HEADS * HD].astype(BF)
    pairs = total[:, HEADS * HD :].T
    gwk_ref[...] = pairs[: HD // 2].astype(BF)
    gwv_ref[...] = pairs[HD // 2 :].astype(BF)
    rg.to_pair()
    ggc.on_far()
    for k in range(1, 8):
        ga_link.arrived(5 + k, ga2.at[(dp + 8 - k) % 8], core_dev)
    total = ((ga2[0] + ga2[1]) + (ga2[2] + ga2[3])) + ((ga2[4] + ga2[5]) + (ga2[6] + ga2[7]))
    for ch in range(CHUNKS):
        ggain_ref[:, ch * CHUNK : (ch + 1) * CHUNK] = total[ch : ch + 1]
    mean = jnp.zeros((ROWS, 1), F32)
    for h in range(2):
        rg.arrived(h)
        for ch in range(4 * h, 4 * h + 4):
            span = slice(ch * CHUNK, (ch + 1) * CHUNK)
            part = inputs_ref[:, span].astype(F32)
            mean += jnp.sum(rg.chunk(ch) * gain_ref[:, span] * part, axis=-1, keepdims=True)
    mean = mean * (1.0 / (CHUNKS * CHUNK)) * inverse_rms * inverse_rms * inverse_rms
    for ch in range(CHUNKS):
        span = slice(ch * CHUNK, (ch + 1) * CHUNK)
        part = inputs_ref[:, span].astype(F32)
        scaled = rg.chunk(ch) * gain_ref[:, span]
        gin_ref[:, span] = (gout_ref[:, span].astype(F32) + inverse_rms * scaled - part * mean).astype(BF)
    ggc.done(other_core(gc))
    total = None
    for s in range(8):
        term = dot_tn(att[s // 2, s % 2], gc[s].reshape(SEQ, CHUNK))
        total = term if total is None else total + term
    gwo_ref[...] = total.astype(BF)

    for link in (gx, gat, gqk, ggc, cols, ro, rg, kv_link, ga_link):
        link.sent()


def hand_over(*refs):
    src, dst, mid, sem_in, sem_out = refs[:7], refs[7:14], refs[14:21], refs[21], refs[22]
    loads = [pltpu.make_async_copy(src[i], mid[i], sem_in.at[i]) for i in range(7)]
    stores = [pltpu.make_async_copy(mid[i], dst[i], sem_out.at[i]) for i in range(7)]
    for cp in loads:
        cp.start()
    for load, store in zip(loads, stores):
        load.wait()
        store.start()
    for cp in stores:
        cp.wait()


def per_device(inputs, gain, doc_ids, w_query, w_key, w_value, w_out, grad_out):
    vmem = pl.BlockSpec(memory_space=pltpu.VMEM)
    hbm = pl.BlockSpec(memory_space=pl.ANY)
    rows = (CHUNKS, 2, 4, 2, ROWS, CHUNK)
    half = (4, 2, ROWS, CHUNK)
    scatter = [
        pltpu.VMEM((CHUNKS, 2, 4, ROWS, CHUNK), BF),
        pltpu.VMEM(half, BF),
        pltpu.VMEM(half, BF),
        pltpu.VMEM((CHUNKS, 2, ROWS, CHUNK), BF),
        pltpu.VMEM((CHUNKS, 2, ROWS, CHUNK), BF),
        pltpu.VMEM((CHUNKS, ROWS, CHUNK), BF),
    ]
    dma = lambda n: [pltpu.SemaphoreType.DMA((n,))] * 2
    outs = pl.pallas_call(
        layer,
        out_shape=(
            jax.ShapeDtypeStruct((ROWS, CHUNKS * CHUNK), BF),
            jax.ShapeDtypeStruct((ROWS, CHUNKS * CHUNK), BF),
            jax.ShapeDtypeStruct((1, CHUNKS * CHUNK), F32),
            jax.ShapeDtypeStruct((CHUNK, HEADS * HD), BF),
            jax.ShapeDtypeStruct((HD // 2, CHUNK), BF),
            jax.ShapeDtypeStruct((HD // 2, CHUNK), BF),
            jax.ShapeDtypeStruct((HEADS * HD, CHUNK), BF),
        ),
        in_specs=[vmem] * 3 + [hbm] * 4 + [vmem],
        out_specs=[vmem] * 7,
        scratch_shapes=[
            pltpu.VMEM(rows, BF),
            pltpu.VMEM(rows, BF),
            pltpu.VMEM(rows, BF),
            pltpu.VMEM(rows, BF),
            pltpu.VMEM(rows, BF),
            pltpu.VMEM((CHUNKS * CHUNK, HEADS * HD), BF),
            pltpu.VMEM((HD, CHUNKS * CHUNK), BF),
            pltpu.VMEM((HEADS * HD, CHUNKS * CHUNK), BF),
            pltpu.VMEM((4, 2, SEQ, HEADS * HD), BF),
            pltpu.VMEM((4, 2, SEQ, HEADS * HD + HD), BF),
            pltpu.VMEM((SEQ, HEADS * HD), F32),
            pltpu.VMEM((2, SEQ, HD), BF),
            pltpu.VMEM((2, 2, SEQ, HD), BF),
            pltpu.VMEM((HEADS, SEQ, HD), BF),
            pltpu.VMEM((HEADS, SEQ, SEQ), F32),
        ]
        + scatter
        + scatter[1:]
        + [
            pltpu.VMEM((4, CHUNKS, CHUNK), F32),
            pltpu.VMEM((4, CHUNKS, CHUNK), F32),
            pltpu.VMEM((8, CHUNKS, CHUNK), F32),
        ]
        + dma(17) * 4
        + dma(9) * 2
        + dma(16) * 2
        + dma(7)
        + dma(2)
        + dma(13)
        + [pltpu.SemaphoreType.DMA((4,))],
        compiler_params=pltpu.CompilerParams(
            collective_id=0, has_side_effects=True, vmem_limit_bytes=60 * 2**20
        ),
    )(
        inputs,
        gain[None, :],
        doc_ids,
        w_query,
        w_key.T,
        w_value.T,
        w_out,
        grad_out,
    )
    out, gin, ggain, gwq, gwk, gwv, gwo = pl.pallas_call(
        hand_over,
        out_shape=[jax.ShapeDtypeStruct(o.shape, o.dtype) for o in outs],
        in_specs=[hbm] * 7,
        out_specs=[hbm] * 7,
        scratch_shapes=[pltpu.VMEM(o.shape, o.dtype) for o in outs] + dma(7),
    )(*outs)
    return (out, gin, ggain.reshape(-1), gwq, gwk.T, gwv.T, gwo)


def solution(mesh):
    return jax.shard_map(
        per_device,
        mesh=mesh,
        in_specs=(
            P(("dp", "head"), None),
            P(),
            P("dp", None),
            P(None, "head"),
            P(None, "head"),
            P(None, "head"),
            P("head", None),
            P(("dp", "head"), None),
        ),
        out_specs=(
            P(("dp", "head"), None),
            P(("dp", "head"), None),
            P(),
            P("dp", "head"),
            P("dp", "head"),
            P("dp", "head"),
            P("head", "dp"),
        ),
        check_vma=False,
    )
```

```python
import math

import jax
import jax.numpy as jnp
from jax import lax
from jax.experimental import pallas as pl
from jax.experimental.pallas import tpu as pltpu
from jax.sharding import PartitionSpec as P

EPSILON = 1e-05
LOG_THETA = math.log(500000.0)
MESH = pl.DeviceIdType.MESH
BF = jnp.bfloat16
F32 = jnp.float32

ROWS = 16
CHUNKS = 8
CHUNK = 1024
SEQ = 256
CUT = 512
HEADS = 4
HD = 128


def device(x, yh, yl, z, c):
    return (x * 2 + yh, (yl * 4 + z) * 2 + c)


def dot(a, b):
    return jnp.dot(a, b, preferred_element_type=F32)


def dot_nt(a, b):
    return lax.dot_general(a, b, (((1,), (1,)), ((), ())), preferred_element_type=F32)


def dot_tn(a, b):
    return lax.dot_general(a, b, (((0,), (0,)), ((), ())), preferred_element_type=F32)


class Link:
    def __init__(self, send, recv):
        self.send, self.recv, self.started = send, recv, []

    def copy(self, k, src, dst, to):
        return pltpu.make_async_remote_copy(
            src_ref=src,
            dst_ref=dst,
            send_sem=self.send.at[k],
            recv_sem=self.recv.at[k],
            device_id=to,
            device_id_type=MESH,
        )

    def start(self, k, src, dst, to):
        cp = self.copy(k, src, dst, to)
        cp.start()
        self.started.append(cp)

    def arrived(self, k, dst, to):
        self.copy(k, dst, dst, to).wait_recv()

    def sent(self):
        for cp in self.started:
            cp.wait_send()
        self.started = []


class Gather:
    def __init__(self, link, slot, half, place, pair, ring, core):
        self.link, self.slot, self.half = link, slot, half
        self.p, self.r = place
        self.pair_dev, self.core_dev = pair, core
        self.next_dev, self.prev_dev = ring
        self.q = 1 - self.p
        self.nxt, self.prv, self.far = (self.r + 1) % 4, (self.r + 3) % 4, (self.r + 2) % 4
        self.shared = []

    def put(self, k, p, r, to):
        ref = self.slot(p, r)
        self.link.start(k, ref, ref, to)

    def put_half(self, k, p, r, h, to):
        ref = self.half(p, r, h)
        self.link.start(k, ref, ref, to)

    def got(self, k, p, r):
        self.link.arrived(k, self.slot(p, r), self.pair_dev)

    def got_half(self, k, p, r, h):
        self.link.arrived(k, self.half(p, r, h), self.pair_dev)

    def share(self, p, r):
        if self.core_dev is not None:
            self.put(9 + len(self.shared), p, r, self.core_dev)
            self.shared.append((p, r))

    def start_pair(self):
        self.put(0, self.p, self.r, self.pair_dev)

    def start_ring(self):
        self.put(1, self.p, self.r, self.next_dev)
        self.put(2, self.p, self.r, self.prev_dev)
        self.share(self.p, self.r)

    def on_pair(self):
        self.got(0, self.q, self.r)
        self.put(3, self.q, self.r, self.next_dev)
        self.put(4, self.q, self.r, self.prev_dev)
        self.share(self.q, self.r)

    def on_ring(self, p, base, k):
        self.got(base, p, self.prv)
        self.put_half(k, p, self.prv, 0, self.next_dev)
        self.share(p, self.prv)
        self.got(base + 1, p, self.nxt)
        self.put_half(k + 1, p, self.nxt, 1, self.prev_dev)
        self.share(p, self.nxt)

    def on_ring_own(self):
        self.on_ring(self.p, 1, 5)

    def on_ring_pair(self):
        self.on_ring(self.q, 3, 7)

    def on_far(self):
        for p, k in ((self.p, 5), (self.q, 7)):
            self.got_half(k, p, self.far, 0)
            self.got_half(k + 1, p, self.far, 1)
            self.share(p, self.far)

    def last_ring(self):
        self.got(1, self.p, self.prv)
        self.put_half(5, self.p, self.prv, 0, self.next_dev)
        self.put(3, self.p, self.prv, self.pair_dev)
        self.share(self.p, self.prv)
        self.got(2, self.p, self.nxt)
        self.put_half(6, self.p, self.nxt, 1, self.prev_dev)
        self.put(4, self.p, self.nxt, self.pair_dev)
        self.share(self.p, self.nxt)

    def last_far(self):
        self.got_half(5, self.p, self.far, 0)
        self.got_half(6, self.p, self.far, 1)
        self.put(7, self.p, self.far, self.pair_dev)
        self.share(self.p, self.far)

    def last_pair(self):
        for k, r in ((0, self.r), (3, self.prv), (4, self.nxt), (7, self.far)):
            self.got(k, self.q, r)
            self.share(self.q, r)

    def done(self, other_slot=None):
        for i, (p, r) in enumerate(self.shared):
            self.link.arrived(9 + i, other_slot(p, r), self.pair_dev)

    def sent(self):
        self.link.sent()


class Scatter:
    def __init__(self, link, parts, bufs, place, devs):
        self.link, self.parts = link, parts
        self.from_core, self.from_prev_half, self.from_next_half, self.from_prev, self.from_next, self.from_pair = bufs
        self.yl, self.z, self.c = place
        self.core_dev, self.pair_dev, self.next_dev, self.prev_dev = devs
        self.nxt, self.prv, self.far = (self.z + 1) % 4, (self.z + 3) % 4, (self.z + 2) % 4

    def give_core(self, ch):
        self.link.copy(
            ch, self.parts.at[ch, :, :, 1 - self.c], self.from_core.at[ch], self.core_dev
        ).start()

    def add_core(self):
        def step(ch, carry):
            self.link.copy(
                ch, self.parts.at[ch, :, :, 1 - self.c], self.from_core.at[ch], self.core_dev
            ).wait()
            own = self.parts[ch, :, :, self.c].astype(F32)
            self.parts[ch, :, :, self.c] = (own + self.from_core[ch].astype(F32)).astype(BF)
            return carry

        lax.fori_loop(0, CHUNKS, step, 0)

    def half(self, z, h):
        return self.parts.at[4 * h : 4 * h + 4, :, z, self.c]

    def start(self):
        link = self.link
        link.start(8, self.half(self.far, 0), self.from_prev_half, self.next_dev)
        link.start(9, self.half(self.far, 1), self.from_next_half, self.prev_dev)
        link.start(10, self.half(self.nxt, 1), self.from_prev.at[4:8], self.next_dev)
        link.start(11, self.half(self.prv, 0), self.from_next.at[0:4], self.prev_dev)

    def middle(self):
        link = self.link
        link.arrived(8, self.from_prev_half, self.pair_dev)
        for ch in range(4):
            mine = self.parts[ch, :, self.nxt, self.c].astype(F32)
            self.parts[ch, :, self.nxt, self.c] = (mine + self.from_prev_half[ch].astype(F32)).astype(BF)
        link.start(12, self.half(self.nxt, 0), self.from_prev.at[0:4], self.next_dev)
        link.arrived(9, self.from_next_half, self.pair_dev)
        for ch in range(4):
            mine = self.parts[4 + ch, :, self.prv, self.c].astype(F32)
            self.parts[4 + ch, :, self.prv, self.c] = (mine + self.from_next_half[ch].astype(F32)).astype(BF)
        link.start(13, self.half(self.prv, 1), self.from_next.at[4:8], self.prev_dev)

    def to_pair(self):
        link = self.link
        link.arrived(10, self.from_prev.at[4:8], self.pair_dev)
        link.arrived(11, self.from_next.at[0:4], self.pair_dev)
        for k, h in ((12, 0), (13, 1)):
            buf = self.from_prev if h == 0 else self.from_next
            link.arrived(k, buf.at[4 * h : 4 * h + 4], self.pair_dev)
            for ch in range(4 * h, 4 * h + 4):
                total = (
                    self.parts[ch, :, self.z, self.c].astype(F32)
                    + self.from_prev[ch].astype(F32)
                    + self.from_next[ch].astype(F32)
                )
                self.parts[ch, :, self.z, self.c] = total.astype(BF)
            link.start(
                14 + h,
                self.parts.at[4 * h : 4 * h + 4, 1 - self.yl, self.z, self.c],
                self.from_pair.at[4 * h : 4 * h + 4],
                self.pair_dev,
            )

    def arrived(self, h):
        self.link.arrived(14 + h, self.from_pair.at[4 * h : 4 * h + 4], self.pair_dev)

    def chunk(self, ch):
        return self.parts[ch, self.yl, self.z, self.c].astype(F32) + self.from_pair[ch].astype(F32)

    def sent(self):
        self.link.sent()


def layer(
    inputs_ref, gain_ref, doc_ref, wq_hbm, wk_hbm, wv_hbm, wo_hbm, gout_ref,
    out_ref, gin_ref, ggain_ref, gwq_ref, gwk_ref, gwv_ref, gwo_ref,
    xs, gs, nc, gc, po, ms, wq, wkv, wo, att, qkv, acc, kvh, kvg, qh, probs,
    rs0, rs1, rs2, rs3, rs4, rs5, rt1, rt2, rt3, rt4, rt5,
    ga0, ga1, ga2,
    x_s, x_r, g_s, g_r, nc_s, nc_r, gc_s, gc_r, fc_s, fc_r, at_s, at_r, qk_s, qk_r, ro_s, ro_r, rg_s, rg_r,
    tn_s, tn_r, kv_s, kv_r, ga_s, ga_r, w_sem,
):
    dp, head = lax.axis_index("dp"), lax.axis_index("head")
    x, yh = dp // 2, dp % 2
    yl, z, c = head // 8, (head // 2) % 4, head % 2
    core_dev = device(x, yh, yl, z, 1 - c)
    pair_dev = device(x, yh, 1 - yl, z, c)
    z_dev = [device(x, yh, yl, (z + k) % 4, c) for k in range(4)]
    dp_devs = [((dp + k) % 8, head) for k in range(1, 8)]
    x_dev = [device((x + k) % 4, yh, yl, z, c) for k in range(4)]
    yh_dev = device(x, 1 - yh, yl, z, c)
    diag_dev = device(x, yh, 1 - yl, z, 1 - c)

    weights = [
        pltpu.make_async_copy(wq_hbm, wq, w_sem.at[0]),
        pltpu.make_async_copy(wk_hbm, wkv.at[0 : HD // 2], w_sem.at[1]),
        pltpu.make_async_copy(wv_hbm, wkv.at[HD // 2 : HD], w_sem.at[2]),
        pltpu.make_async_copy(wo_hbm, wo, w_sem.at[3]),
    ]
    for cp in weights:
        cp.start()

    barrier = pltpu.get_barrier_semaphore()
    partners = [core_dev, pair_dev, diag_dev] + z_dev[1:] + dp_devs
    for to in partners:
        pl.semaphore_signal(barrier, inc=1, device_id=to, device_id_type=MESH)

    square = jnp.zeros((ROWS, 1), F32)
    for ch in range(CHUNKS):
        part = inputs_ref[:, ch * CHUNK : (ch + 1) * CHUNK].astype(F32)
        square += jnp.sum(part * part, axis=-1, keepdims=True)
    inverse_rms = lax.rsqrt(square * (1.0 / (CHUNKS * CHUNK)) + EPSILON)
    for ch in range(CHUNKS):
        cols = slice(ch * CHUNK, (ch + 1) * CHUNK)
        part = inputs_ref[:, cols].astype(F32)
        xs[ch, yl, z, c] = (part * inverse_rms * gain_ref[:, cols]).astype(BF)
        gs[ch, yl, z, c] = gout_ref[:, cols]
    gc[dp, yl, z, c] = gs[dp, yl, z, c]

    pl.semaphore_wait(barrier, len(partners))

    def head_gather(buf, send, recv):
        return Gather(
            Link(send, recv),
            lambda p, r: buf.at[:, p, r, c],
            lambda p, r, h: buf.at[4 * h : 4 * h + 4, p, r, c],
            (yl, z), pair_dev, (z_dev[1], z_dev[3]), core_dev,
        )

    def other_core(buf):
        return lambda p, r: buf.at[:, p, r, 1 - c]

    def dp_gather(buf, send, recv):
        return Gather(
            Link(send, recv),
            lambda p, r: buf.at[r, p],
            lambda p, r, h: buf.at[r, p, 128 * h : 128 * h + 128],
            (yh, x), yh_dev, (x_dev[1], x_dev[3]), None,
        )

    gx, gg = head_gather(xs, x_s, x_r), head_gather(gs, g_s, g_r)
    near_cols = gc.at[:, :, :, :, :, 0:CUT]
    ggc = head_gather(near_cols, gc_s, gc_r)
    cols = Link(nc_s, nc_r)
    far_cols = Link(fc_s, fc_r)
    gat, gqk = dp_gather(att, at_s, at_r), dp_gather(qkv, qk_s, qk_r)
    devs = (core_dev, pair_dev, z_dev[1], z_dev[3])
    ro = Scatter(Link(ro_s, ro_r), po, (rs0, rs1, rs2, rs3, rs4, rs5), (yl, z, c), devs)
    rg = Scatter(Link(rg_s, rg_r), gs, (rs0, rt1, rt2, rt3, rt4, rt5), (yl, z, c), devs)

    gx.start_ring()
    gx.start_pair()
    tiny = Link(tn_s, tn_r)
    for k in range(1, 8):
        to = (dp + k) % 8
        tiny.start(k - 1, gs.at[to, yl, z, c, :, 0:CUT], gc.at[dp, yl, z, c, :, 0:CUT], (to, head))

    row_index = lax.broadcasted_iota(jnp.int32, (SEQ, SEQ), 0)
    col_index = lax.broadcasted_iota(jnp.int32, (SEQ, SEQ), 1)
    doc_rows = jnp.broadcast_to(doc_ref[...].astype(F32), (SEQ, SEQ))
    same = doc_rows == doc_rows.T
    allowed = same & (col_index <= row_index)
    position = jnp.sum(jnp.where(allowed, 1.0, 0.0), axis=-1, keepdims=True) - 1.0
    lane = lax.broadcasted_iota(jnp.int32, (SEQ, HD), 1)
    low_half = lane < HD // 2
    exponent = jnp.where(low_half, lane, lane - HD // 2).astype(F32) * (2.0 / HD)
    angles = position * jnp.exp(exponent * -LOG_THETA)
    cosine, sine = jnp.cos(angles), jnp.sin(angles)
    sine_turn = jnp.where(low_half, -sine, sine)

    def rope(u):
        return u * cosine + pltpu.roll(u, HD // 2, 1) * sine_turn

    def rope_back(g):
        turned = pltpu.roll(g * sine, HD // 2, 1)
        return g * cosine + jnp.where(low_half, turned, -turned)

    spots = [
        (yl, z), (1 - yl, z), (yl, gx.prv), (yl, gx.nxt),
        (1 - yl, gx.prv), (1 - yl, gx.nxt), (yl, gx.far), (1 - yl, gx.far),
    ]

    def spread_copy(i, k):
        p, r = spots[i]
        to = (dp + k) % 8
        return cols.copy(7 * i + k - 1, xs.at[to, p, r, c], nc.at[dp, p, r, c], (to, head))

    def spread(*blocks):
        def step(k, carry):
            for i in blocks:
                spread_copy(i, k).start()
            return carry

        lax.fori_loop(1, 8, step, 0)

    def spread_share(k):
        block = nc.at[(dp + 8 - k) % 8, :, :, c]
        return cols.copy(55 + k, block, block, core_dev)

    def collect(k, carry):
        for i in range(8):
            p, r = spots[i]
            cols.arrived(7 * i + k - 1, nc.at[(dp + 8 - k) % 8, p, r, c], core_dev)
        spread_share(k).start()
        return carry

    def collected(k, carry):
        cols.arrived(55 + k, nc.at[(dp + 8 - k) % 8, :, :, 1 - c], core_dev)
        return carry

    def spread_sent(k, carry):
        for i in range(8):
            spread_copy(i, k).wait_send()
        spread_share(k).wait_send()
        return carry

    spread(0)
    gx.on_pair()
    gg.start_pair()
    spread(1)
    gx.on_ring_own()
    spread(2, 3)
    gx.on_ring_pair()
    spread(4, 5)
    gg.start_ring()
    gg.on_pair()
    gx.on_far()
    spread(6, 7)
    gx.done(other_core(xs))
    nc[dp] = xs[dp]

    for cp in weights[:3]:
        cp.wait()

    def project(ch, carry):
        block = xs[ch].reshape(SEQ, CHUNK)
        rows = pl.ds(pl.multiple_of(ch * CHUNK, CHUNK), CHUNK)
        acc[...] += dot(block, wq[rows, :])
        kvh_acc[...] += dot_nt(block, wkv[:, rows])
        return carry

    kvh_acc = probs.at[0, :, 0:HD]
    acc[...] = jnp.zeros_like(acc)
    kvh_acc[...] = jnp.zeros((SEQ, HD), F32)
    lax.fori_loop(0, CHUNKS, project, 0)
    kvh[c] = kvh_acc[...].astype(BF)
    kv_link = Link(kv_s, kv_r)
    kv_link.start(0, kvh.at[c], kvh.at[c], core_dev)
    gg.on_ring_own()
    for h in range(HEADS):
        pre = acc[:, h * HD : (h + 1) * HD].astype(BF).astype(F32)
        qh[h] = rope(pre).astype(BF)
    kv_link.arrived(0, kvh.at[1 - c], core_dev)
    first, second = kvh[0].astype(F32), kvh[1].astype(F32)
    key_pre = jnp.where(low_half, first, pltpu.roll(second, HD // 2, 1))
    values = jnp.where(low_half, pltpu.roll(first, HD // 2, 1), second).astype(BF)
    key_rows = rope(key_pre).astype(BF)
    score_scale = HD ** (-0.5)

    for h in range(HEADS):
        scores = dot_nt(qh[h], key_rows) * score_scale
        scores = jnp.where(allowed, scores, -1e30)
        top = jnp.max(scores, axis=-1, keepdims=True)
        e = jnp.exp(scores - top)
        p = e / jnp.sum(e, axis=-1, keepdims=True)
        probs[h] = p
        att[x, yh, :, h * HD : (h + 1) * HD] = dot(p.astype(BF), values).astype(BF)
    gat.start_ring()
    gat.start_pair()
    gg.on_ring_pair()

    weights[3].wait()
    wide = (2, 4, 2, ROWS, CHUNK)

    def project_out(ch, carry):
        cols_ch = pl.ds(pl.multiple_of(ch * CHUNK, CHUNK), CHUNK)
        po[ch] = dot(att[x, yh], wo[:, cols_ch]).astype(BF).reshape(wide)
        ro.give_core(ch)
        return carry

    lax.fori_loop(0, CHUNKS, project_out, 0)
    ro.add_core()
    gg.on_far()
    for k in range(1, 8):
        tiny.arrived(k - 1, gc.at[(dp + 8 - k) % 8, yl, z, c, :, 0:CUT], core_dev)
    ggc.start_ring()
    ggc.start_pair()
    ro.start()
    gat.on_pair()
    gg.done(other_core(gs))
    for ch in range(CHUNKS):
        ms[ch] = gs[ch, :, :, c, :, CUT:]
    for k in range(1, 8):
        to = (dp + k) % 8
        far_cols.start(k - 1, ms.at[to], gc.at[dp, :, :, c, :, CUT:], (to, head))
    gc[dp, :, :, :, :, CUT:] = gs[dp, :, :, :, :, CUT:]
    lax.fori_loop(1, 8, collect, 0)

    acc[...] = jnp.zeros_like(acc)

    def back_out(ch, carry):
        cols_ch = pl.ds(pl.multiple_of(ch * CHUNK, CHUNK), CHUNK)
        acc[...] += dot_nt(gs[ch].reshape(SEQ, CHUNK), wo[:, cols_ch])
        return carry

    lax.fori_loop(0, CHUNKS, back_out, 0)
    gat.on_ring_own()
    ggc.on_pair()
    key_sum = jnp.zeros((SEQ, HD), F32)
    value_sum = jnp.zeros((SEQ, HD), F32)
    for h in range(HEADS):
        grad_att = acc[:, h * HD : (h + 1) * HD].astype(BF)
        p = probs[h]
        grad_probs = dot_nt(grad_att, values)
        delta = jnp.sum(p * grad_probs, axis=-1, keepdims=True)
        grad_scores = (p * (grad_probs - delta)).astype(BF)
        grad_query = dot(grad_scores, key_rows) * score_scale
        qkv[x, yh, :, h * HD : (h + 1) * HD] = rope_back(grad_query).astype(BF)
        key_sum += dot_tn(grad_scores, qh[h])
        value_sum += dot_tn(p.astype(BF), grad_att)
    kvg[c, 0] = rope_back(key_sum * score_scale).astype(BF)
    kvg[c, 1] = value_sum.astype(BF)
    kv_link.start(1, kvg.at[c], kvg.at[c], core_dev)
    ro.middle()
    kv_link.arrived(1, kvg.at[1 - c], core_dev)
    key_pair = (kvg[0, 0].astype(F32) + kvg[1, 0].astype(F32)).astype(BF).astype(F32)
    value_pair = (kvg[0, 1].astype(F32) + kvg[1, 1].astype(F32)).astype(BF).astype(F32)
    even = jnp.where(low_half, key_pair, pltpu.roll(value_pair, HD // 2, 1))
    odd = jnp.where(low_half, pltpu.roll(key_pair, HD // 2, 1), value_pair)
    qkv[x, yh, :, HEADS * HD :] = jnp.where(c == 0, even, odd).astype(BF)
    gqk.start_ring()
    gqk.start_pair()
    gat.on_ring_pair()
    ggc.on_ring_own()
    gg.sent()
    tiny.sent()

    def back_in(ch, carry):
        rows = pl.ds(pl.multiple_of(ch * CHUNK, CHUNK), CHUNK)
        part = dot_nt(qkv[x, yh, :, : HEADS * HD], wq[rows, :])
        part += dot(qkv[x, yh, :, HEADS * HD :], wkv[:, rows])
        gs[ch] = part.astype(BF).reshape(wide)
        rg.give_core(ch)
        return carry

    lax.fori_loop(0, CHUNKS, back_in, 0)
    rg.add_core()
    rg.start()

    gain_slot = yl * 2 + c
    for ch in range(CHUNKS):
        term = gs[ch, :, :, c].astype(F32) * xs[ch, :, :, c].astype(F32)
        term = jnp.sum(term.reshape(SEQ // 2, CHUNK), axis=0, keepdims=True)
        ga0[gain_slot, ch : ch + 1] = term / gain_ref[:, ch * CHUNK : (ch + 1) * CHUNK]
    ga_link = Link(ga_s, ga_r)
    near = [(core_dev, yl * 2 + 1 - c), (pair_dev, (1 - yl) * 2 + c), (diag_dev, (1 - yl) * 2 + 1 - c)]
    for k, (to, _) in enumerate(near):
        ga_link.start(k, ga0.at[gain_slot], ga0.at[gain_slot], to)

    gqk.on_pair()
    gqk.on_ring_own()
    ro.to_pair()
    for k, (_, slot) in enumerate(near):
        ga_link.arrived(k, ga0.at[slot], core_dev)
    ga1[z] = (ga0[0] + ga0[1]) + (ga0[2] + ga0[3])
    for k in range(1, 4):
        ga_link.start(2 + k, ga1.at[z], ga1.at[z], z_dev[k])
    gat.on_far()
    rg.middle()
    ggc.on_ring_pair()
    for h in range(2):
        ro.arrived(h)
        for ch in range(4 * h, 4 * h + 4):
            span = slice(ch * CHUNK, (ch + 1) * CHUNK)
            out_ref[:, span] = (inputs_ref[:, span].astype(F32) + ro.chunk(ch)).astype(BF)
    gqk.on_ring_pair()
    for k in range(1, 8):
        block = gc.at[(dp + 8 - k) % 8, :, :, c, :, CUT:]
        far_cols.arrived(k - 1, block, core_dev)
        far_cols.start(6 + k, block, block, core_dev)
    for k in range(1, 4):
        ga_link.arrived(2 + k, ga1.at[(z + 4 - k) % 4], core_dev)
    ga2[dp] = (ga1[0] + ga1[1]) + (ga1[2] + ga1[3])
    for k in range(1, 8):
        ga_link.start(5 + k, ga2.at[dp], ga2.at[dp], ((dp + k) % 8, head))

    lax.fori_loop(1, 8, collected, 0)
    rg.to_pair()
    gqk.on_far()
    total = None
    for s in range(8):
        term = dot_tn(nc[s].reshape(SEQ, CHUNK), qkv[s // 2, s % 2])
        total = term if total is None else total + term
    gwq_ref[...] = total[:, : HEADS * HD].astype(BF)
    pairs = total[:, HEADS * HD :].T
    gwk_ref[...] = pairs[: HD // 2].astype(BF)
    gwv_ref[...] = pairs[HD // 2 :].astype(BF)
    ggc.on_far()
    for k in range(1, 8):
        ga_link.arrived(5 + k, ga2.at[(dp + 8 - k) % 8], core_dev)
    total = ((ga2[0] + ga2[1]) + (ga2[2] + ga2[3])) + ((ga2[4] + ga2[5]) + (ga2[6] + ga2[7]))
    for ch in range(CHUNKS):
        ggain_ref[:, ch * CHUNK : (ch + 1) * CHUNK] = total[ch : ch + 1]
    mean = jnp.zeros((ROWS, 1), F32)
    for h in range(2):
        rg.arrived(h)
        for ch in range(4 * h, 4 * h + 4):
            span = slice(ch * CHUNK, (ch + 1) * CHUNK)
            part = inputs_ref[:, span].astype(F32)
            mean += jnp.sum(rg.chunk(ch) * gain_ref[:, span] * part, axis=-1, keepdims=True)
    mean = mean * (1.0 / (CHUNKS * CHUNK)) * inverse_rms * inverse_rms * inverse_rms
    for ch in range(CHUNKS):
        span = slice(ch * CHUNK, (ch + 1) * CHUNK)
        part = inputs_ref[:, span].astype(F32)
        scaled = rg.chunk(ch) * gain_ref[:, span]
        gin_ref[:, span] = (gout_ref[:, span].astype(F32) + inverse_rms * scaled - part * mean).astype(BF)
    ggc.done(other_core(near_cols))
    for k in range(1, 8):
        far_cols.arrived(6 + k, gc.at[(dp + 8 - k) % 8, :, :, 1 - c, :, CUT:], core_dev)
    total = None
    for s in range(8):
        term = dot_tn(att[s // 2, s % 2], gc[s].reshape(SEQ, CHUNK))
        total = term if total is None else total + term
    gwo_ref[...] = total.astype(BF)

    lax.fori_loop(1, 8, spread_sent, 0)
    for link in (gx, gat, gqk, ggc, far_cols, ro, rg, kv_link, ga_link):
        link.sent()


def hand_over(*refs):
    src, dst, mid, sem_in, sem_out = refs[:7], refs[7:14], refs[14:21], refs[21], refs[22]
    loads = [pltpu.make_async_copy(src[i], mid[i], sem_in.at[i]) for i in range(7)]
    stores = [pltpu.make_async_copy(mid[i], dst[i], sem_out.at[i]) for i in range(7)]
    for cp in loads:
        cp.start()
    for load, store in zip(loads, stores):
        load.wait()
        store.start()
    for cp in stores:
        cp.wait()


def per_device(inputs, gain, doc_ids, w_query, w_key, w_value, w_out, grad_out):
    vmem = pl.BlockSpec(memory_space=pltpu.VMEM)
    hbm = pl.BlockSpec(memory_space=pl.ANY)
    rows = (CHUNKS, 2, 4, 2, ROWS, CHUNK)
    half = (4, 2, ROWS, CHUNK)
    scatter = [
        pltpu.VMEM((CHUNKS, 2, 4, ROWS, CHUNK), BF),
        pltpu.VMEM(half, BF),
        pltpu.VMEM(half, BF),
        pltpu.VMEM((CHUNKS, 2, ROWS, CHUNK), BF),
        pltpu.VMEM((CHUNKS, 2, ROWS, CHUNK), BF),
        pltpu.VMEM((CHUNKS, ROWS, CHUNK), BF),
    ]
    dma = lambda n: [pltpu.SemaphoreType.DMA((n,))] * 2
    outs = pl.pallas_call(
        layer,
        out_shape=(
            jax.ShapeDtypeStruct((ROWS, CHUNKS * CHUNK), BF),
            jax.ShapeDtypeStruct((ROWS, CHUNKS * CHUNK), BF),
            jax.ShapeDtypeStruct((1, CHUNKS * CHUNK), F32),
            jax.ShapeDtypeStruct((CHUNK, HEADS * HD), BF),
            jax.ShapeDtypeStruct((HD // 2, CHUNK), BF),
            jax.ShapeDtypeStruct((HD // 2, CHUNK), BF),
            jax.ShapeDtypeStruct((HEADS * HD, CHUNK), BF),
        ),
        in_specs=[vmem] * 3 + [hbm] * 4 + [vmem],
        out_specs=[vmem] * 7,
        scratch_shapes=[
            pltpu.VMEM(rows, BF),
            pltpu.VMEM(rows, BF),
            pltpu.VMEM(rows, BF),
            pltpu.VMEM(rows, BF),
            pltpu.VMEM(rows, BF),
            pltpu.VMEM((CHUNKS, 2, 4, ROWS, CHUNK - CUT), BF),
            pltpu.VMEM((CHUNKS * CHUNK, HEADS * HD), BF),
            pltpu.VMEM((HD, CHUNKS * CHUNK), BF),
            pltpu.VMEM((HEADS * HD, CHUNKS * CHUNK), BF),
            pltpu.VMEM((4, 2, SEQ, HEADS * HD), BF),
            pltpu.VMEM((4, 2, SEQ, HEADS * HD + HD), BF),
            pltpu.VMEM((SEQ, HEADS * HD), F32),
            pltpu.VMEM((2, SEQ, HD), BF),
            pltpu.VMEM((2, 2, SEQ, HD), BF),
            pltpu.VMEM((HEADS, SEQ, HD), BF),
            pltpu.VMEM((HEADS, SEQ, SEQ), F32),
        ]
        + scatter
        + scatter[1:]
        + [
            pltpu.VMEM((4, CHUNKS, CHUNK), F32),
            pltpu.VMEM((4, CHUNKS, CHUNK), F32),
            pltpu.VMEM((8, CHUNKS, CHUNK), F32),
        ]
        + dma(17) * 2
        + dma(63)
        + dma(17)
        + dma(14)
        + dma(9) * 2
        + dma(16) * 2
        + dma(7)
        + dma(2)
        + dma(13)
        + [pltpu.SemaphoreType.DMA((4,))],
        compiler_params=pltpu.CompilerParams(
            collective_id=0, has_side_effects=True, vmem_limit_bytes=62 * 2**20
        ),
    )(
        inputs,
        gain[None, :],
        doc_ids,
        w_query,
        w_key.T,
        w_value.T,
        w_out,
        grad_out,
    )
    out, gin, ggain, gwq, gwk, gwv, gwo = pl.pallas_call(
        hand_over,
        out_shape=[jax.ShapeDtypeStruct(o.shape, o.dtype) for o in outs],
        in_specs=[hbm] * 7,
        out_specs=[hbm] * 7,
        scratch_shapes=[pltpu.VMEM(o.shape, o.dtype) for o in outs] + dma(7),
    )(*outs)
    return (out, gin, ggain.reshape(-1), gwq, gwk.T, gwv.T, gwo)


def solution(mesh):
    return jax.shard_map(
        per_device,
        mesh=mesh,
        in_specs=(
            P(("dp", "head"), None),
            P(),
            P("dp", None),
            P(None, "head"),
            P(None, "head"),
            P(None, "head"),
            P("head", None),
            P(("dp", "head"), None),
        ),
        out_specs=(
            P(("dp", "head"), None),
            P(("dp", "head"), None),
            P(),
            P("dp", "head"),
            P("dp", "head"),
            P("dp", "head"),
            P("head", "dp"),
        ),
        check_vma=False,
    )
```

```python
import math

import jax
import jax.numpy as jnp
from jax import lax
from jax.experimental import pallas as pl
from jax.experimental.pallas import tpu as pltpu
from jax.sharding import PartitionSpec as P

EPSILON = 1e-05
LOG_THETA = math.log(500000.0)
MESH = pl.DeviceIdType.MESH
BF = jnp.bfloat16
F32 = jnp.float32

ROWS = 16
CHUNKS = 8
CHUNK = 1024
SEQ = 256
CUT = 768
HEADS = 4
HD = 128


def device(x, yh, yl, z, c):
    return (x * 2 + yh, (yl * 4 + z) * 2 + c)


def dot(a, b):
    return jnp.dot(a, b, preferred_element_type=F32)


def dot_nt(a, b):
    return lax.dot_general(a, b, (((1,), (1,)), ((), ())), preferred_element_type=F32)


def dot_tn(a, b):
    return lax.dot_general(a, b, (((0,), (0,)), ((), ())), preferred_element_type=F32)


class Link:
    def __init__(self, send, recv):
        self.send, self.recv, self.started = send, recv, []

    def copy(self, k, src, dst, to):
        return pltpu.make_async_remote_copy(
            src_ref=src,
            dst_ref=dst,
            send_sem=self.send.at[k],
            recv_sem=self.recv.at[k],
            device_id=to,
            device_id_type=MESH,
        )

    def start(self, k, src, dst, to):
        cp = self.copy(k, src, dst, to)
        cp.start()
        self.started.append(cp)

    def arrived(self, k, dst, to):
        self.copy(k, dst, dst, to).wait_recv()

    def sent(self):
        for cp in self.started:
            cp.wait_send()
        self.started = []


class Gather:
    def __init__(self, link, slot, half, place, pair, ring, core):
        self.link, self.slot, self.half = link, slot, half
        self.p, self.r = place
        self.pair_dev, self.core_dev = pair, core
        self.next_dev, self.prev_dev = ring
        self.q = 1 - self.p
        self.nxt, self.prv, self.far = (self.r + 1) % 4, (self.r + 3) % 4, (self.r + 2) % 4
        self.shared = []

    def put(self, k, p, r, to):
        ref = self.slot(p, r)
        self.link.start(k, ref, ref, to)

    def put_half(self, k, p, r, h, to):
        ref = self.half(p, r, h)
        self.link.start(k, ref, ref, to)

    def got(self, k, p, r):
        self.link.arrived(k, self.slot(p, r), self.pair_dev)

    def got_half(self, k, p, r, h):
        self.link.arrived(k, self.half(p, r, h), self.pair_dev)

    def share(self, p, r):
        if self.core_dev is not None:
            self.put(9 + len(self.shared), p, r, self.core_dev)
            self.shared.append((p, r))

    def start_pair(self):
        self.put(0, self.p, self.r, self.pair_dev)

    def start_ring(self):
        self.put(1, self.p, self.r, self.next_dev)
        self.put(2, self.p, self.r, self.prev_dev)
        self.share(self.p, self.r)

    def on_pair(self):
        self.got(0, self.q, self.r)
        self.put(3, self.q, self.r, self.next_dev)
        self.put(4, self.q, self.r, self.prev_dev)
        self.share(self.q, self.r)

    def on_ring(self, p, base, k):
        self.got(base, p, self.prv)
        self.put_half(k, p, self.prv, 0, self.next_dev)
        self.share(p, self.prv)
        self.got(base + 1, p, self.nxt)
        self.put_half(k + 1, p, self.nxt, 1, self.prev_dev)
        self.share(p, self.nxt)

    def on_ring_own(self):
        self.on_ring(self.p, 1, 5)

    def on_ring_pair(self):
        self.on_ring(self.q, 3, 7)

    def on_far(self):
        for p, k in ((self.p, 5), (self.q, 7)):
            self.got_half(k, p, self.far, 0)
            self.got_half(k + 1, p, self.far, 1)
            self.share(p, self.far)

    def last_ring(self):
        self.got(1, self.p, self.prv)
        self.put_half(5, self.p, self.prv, 0, self.next_dev)
        self.put(3, self.p, self.prv, self.pair_dev)
        self.share(self.p, self.prv)
        self.got(2, self.p, self.nxt)
        self.put_half(6, self.p, self.nxt, 1, self.prev_dev)
        self.put(4, self.p, self.nxt, self.pair_dev)
        self.share(self.p, self.nxt)

    def last_far(self):
        self.got_half(5, self.p, self.far, 0)
        self.got_half(6, self.p, self.far, 1)
        self.put(7, self.p, self.far, self.pair_dev)
        self.share(self.p, self.far)

    def last_pair(self):
        for k, r in ((0, self.r), (3, self.prv), (4, self.nxt), (7, self.far)):
            self.got(k, self.q, r)
            self.share(self.q, r)

    def done(self, other_slot=None):
        for i, (p, r) in enumerate(self.shared):
            self.link.arrived(9 + i, other_slot(p, r), self.pair_dev)

    def sent(self):
        self.link.sent()


class Scatter:
    def __init__(self, link, parts, bufs, place, devs):
        self.link, self.parts = link, parts
        self.from_core, self.from_prev_half, self.from_next_half, self.from_prev, self.from_next, self.from_pair = bufs
        self.yl, self.z, self.c = place
        self.core_dev, self.pair_dev, self.next_dev, self.prev_dev = devs
        self.nxt, self.prv, self.far = (self.z + 1) % 4, (self.z + 3) % 4, (self.z + 2) % 4

    def give_core(self, ch):
        self.link.copy(
            ch, self.parts.at[ch, :, :, 1 - self.c], self.from_core.at[ch], self.core_dev
        ).start()

    def add_core(self, ch):
        self.link.copy(
            ch, self.parts.at[ch, :, :, 1 - self.c], self.from_core.at[ch], self.core_dev
        ).wait()
        own = self.parts[ch, :, :, self.c].astype(F32)
        self.parts[ch, :, :, self.c] = (own + self.from_core[ch].astype(F32)).astype(BF)

    def run(self, make):
        half = CHUNKS // 2

        def first(ch, carry):
            make(ch)
            return carry

        def second(ch, carry):
            make(ch)
            self.add_core(ch - half)
            return carry

        def rest(ch, carry):
            self.add_core(ch)
            return carry

        lax.fori_loop(0, half, first, 0)
        lax.fori_loop(half, CHUNKS, second, 0)
        self.start_low()
        lax.fori_loop(half, CHUNKS, rest, 0)
        self.start_high()

    def half(self, z, h):
        return self.parts.at[4 * h : 4 * h + 4, :, z, self.c]

    def start_low(self):
        link = self.link
        link.start(8, self.half(self.far, 0), self.from_prev_half, self.next_dev)
        link.start(11, self.half(self.prv, 0), self.from_next.at[0:4], self.prev_dev)

    def start_high(self):
        link = self.link
        link.start(9, self.half(self.far, 1), self.from_next_half, self.prev_dev)
        link.start(10, self.half(self.nxt, 1), self.from_prev.at[4:8], self.next_dev)

    def middle(self):
        link = self.link
        link.arrived(8, self.from_prev_half, self.pair_dev)
        for ch in range(4):
            mine = self.parts[ch, :, self.nxt, self.c].astype(F32)
            self.parts[ch, :, self.nxt, self.c] = (mine + self.from_prev_half[ch].astype(F32)).astype(BF)
        link.start(12, self.half(self.nxt, 0), self.from_prev.at[0:4], self.next_dev)
        link.arrived(9, self.from_next_half, self.pair_dev)
        for ch in range(4):
            mine = self.parts[4 + ch, :, self.prv, self.c].astype(F32)
            self.parts[4 + ch, :, self.prv, self.c] = (mine + self.from_next_half[ch].astype(F32)).astype(BF)
        link.start(13, self.half(self.prv, 1), self.from_next.at[4:8], self.prev_dev)

    def to_pair(self):
        link = self.link
        link.arrived(10, self.from_prev.at[4:8], self.pair_dev)
        link.arrived(11, self.from_next.at[0:4], self.pair_dev)
        for k, h in ((12, 0), (13, 1)):
            buf = self.from_prev if h == 0 else self.from_next
            link.arrived(k, buf.at[4 * h : 4 * h + 4], self.pair_dev)
            for ch in range(4 * h, 4 * h + 4):
                total = (
                    self.parts[ch, :, self.z, self.c].astype(F32)
                    + self.from_prev[ch].astype(F32)
                    + self.from_next[ch].astype(F32)
                )
                self.parts[ch, :, self.z, self.c] = total.astype(BF)
            link.start(
                14 + h,
                self.parts.at[4 * h : 4 * h + 4, 1 - self.yl, self.z, self.c],
                self.from_pair.at[4 * h : 4 * h + 4],
                self.pair_dev,
            )

    def arrived(self, h):
        self.link.arrived(14 + h, self.from_pair.at[4 * h : 4 * h + 4], self.pair_dev)

    def chunk(self, ch):
        return self.parts[ch, self.yl, self.z, self.c].astype(F32) + self.from_pair[ch].astype(F32)

    def sent(self):
        self.link.sent()


def layer(
    inputs_ref, gain_ref, doc_ref, wq_hbm, wk_hbm, wv_hbm, wo_hbm, gout_ref,
    out_ref, gin_ref, ggain_ref, gwq_ref, gwk_ref, gwv_ref, gwo_ref,
    xs, gs, nc, gc, po, ms, wq, wkv, wo, att, qkv, acc, kvh, kvg, qh, probs,
    rs0, rs1, rs2, rs3, rs4, rs5, rt1, rt2, rt3, rt4, rt5,
    ga0, ga1, ga2,
    x_s, x_r, g_s, g_r, nc_s, nc_r, gc_s, gc_r, fc_s, fc_r, at_s, at_r, qk_s, qk_r, ro_s, ro_r, rg_s, rg_r,
    tn_s, tn_r, kv_s, kv_r, ga_s, ga_r, w_sem,
):
    dp, head = lax.axis_index("dp"), lax.axis_index("head")
    x, yh = dp // 2, dp % 2
    yl, z, c = head // 8, (head // 2) % 4, head % 2
    core_dev = device(x, yh, yl, z, 1 - c)
    pair_dev = device(x, yh, 1 - yl, z, c)
    z_dev = [device(x, yh, yl, (z + k) % 4, c) for k in range(4)]
    dp_devs = [((dp + k) % 8, head) for k in range(1, 8)]
    x_dev = [device((x + k) % 4, yh, yl, z, c) for k in range(4)]
    yh_dev = device(x, 1 - yh, yl, z, c)
    diag_dev = device(x, yh, 1 - yl, z, 1 - c)

    weights = [
        pltpu.make_async_copy(wq_hbm, wq, w_sem.at[0]),
        pltpu.make_async_copy(wk_hbm, wkv.at[0 : HD // 2], w_sem.at[1]),
        pltpu.make_async_copy(wv_hbm, wkv.at[HD // 2 : HD], w_sem.at[2]),
        pltpu.make_async_copy(wo_hbm, wo, w_sem.at[3]),
    ]
    for cp in weights:
        cp.start()

    barrier = pltpu.get_barrier_semaphore()
    partners = [core_dev, pair_dev, diag_dev] + z_dev[1:] + dp_devs
    for to in partners:
        pl.semaphore_signal(barrier, inc=1, device_id=to, device_id_type=MESH)

    square = jnp.zeros((ROWS, 1), F32)
    for ch in range(CHUNKS):
        part = inputs_ref[:, ch * CHUNK : (ch + 1) * CHUNK].astype(F32)
        square += jnp.sum(part * part, axis=-1, keepdims=True)
    inverse_rms = lax.rsqrt(square * (1.0 / (CHUNKS * CHUNK)) + EPSILON)
    for ch in range(CHUNKS):
        cols = slice(ch * CHUNK, (ch + 1) * CHUNK)
        part = inputs_ref[:, cols].astype(F32)
        xs[ch, yl, z, c] = (part * inverse_rms * gain_ref[:, cols]).astype(BF)
        gs[ch, yl, z, c] = gout_ref[:, cols]
    gc[dp, yl, z, c] = gs[dp, yl, z, c]

    pl.semaphore_wait(barrier, len(partners))

    def head_gather(buf, send, recv):
        return Gather(
            Link(send, recv),
            lambda p, r: buf.at[:, p, r, c],
            lambda p, r, h: buf.at[4 * h : 4 * h + 4, p, r, c],
            (yl, z), pair_dev, (z_dev[1], z_dev[3]), core_dev,
        )

    def other_core(buf):
        return lambda p, r: buf.at[:, p, r, 1 - c]

    def dp_gather(buf, send, recv):
        return Gather(
            Link(send, recv),
            lambda p, r: buf.at[r, p],
            lambda p, r, h: buf.at[r, p, 128 * h : 128 * h + 128],
            (yh, x), yh_dev, (x_dev[1], x_dev[3]), None,
        )

    gx, gg = head_gather(xs, x_s, x_r), head_gather(gs, g_s, g_r)
    near_cols = gc.at[:, :, :, :, :, 0:CUT]
    ggc = head_gather(near_cols, gc_s, gc_r)
    cols = Link(nc_s, nc_r)
    far_cols = Link(fc_s, fc_r)
    gat, gqk = dp_gather(att, at_s, at_r), dp_gather(qkv, qk_s, qk_r)
    devs = (core_dev, pair_dev, z_dev[1], z_dev[3])
    ro = Scatter(Link(ro_s, ro_r), po, (rs0, rs1, rs2, rs3, rs4, rs5), (yl, z, c), devs)
    rg = Scatter(Link(rg_s, rg_r), gs, (rs0, rt1, rt2, rt3, rt4, rt5), (yl, z, c), devs)

    gx.start_ring()
    gx.start_pair()
    tiny = Link(tn_s, tn_r)
    for k in range(1, 8):
        to = (dp + k) % 8
        tiny.start(k - 1, gs.at[to, yl, z, c, :, 0:CUT], gc.at[dp, yl, z, c, :, 0:CUT], (to, head))

    row_index = lax.broadcasted_iota(jnp.int32, (SEQ, SEQ), 0)
    col_index = lax.broadcasted_iota(jnp.int32, (SEQ, SEQ), 1)
    doc_rows = jnp.broadcast_to(doc_ref[...].astype(F32), (SEQ, SEQ))
    same = doc_rows == doc_rows.T
    allowed = same & (col_index <= row_index)
    position = jnp.sum(jnp.where(allowed, 1.0, 0.0), axis=-1, keepdims=True) - 1.0
    lane = lax.broadcasted_iota(jnp.int32, (SEQ, HD), 1)
    low_half = lane < HD // 2
    exponent = jnp.where(low_half, lane, lane - HD // 2).astype(F32) * (2.0 / HD)
    angles = position * jnp.exp(exponent * -LOG_THETA)
    cosine, sine = jnp.cos(angles), jnp.sin(angles)
    sine_turn = jnp.where(low_half, -sine, sine)

    def rope(u):
        return u * cosine + pltpu.roll(u, HD // 2, 1) * sine_turn

    def rope_back(g):
        turned = pltpu.roll(g * sine, HD // 2, 1)
        return g * cosine + jnp.where(low_half, turned, -turned)

    def spread(*places):
        def step(k, carry):
            to = (dp + k) % 8
            for r in places:
                cols.copy(k - 1, xs.at[to, :, r, c], nc.at[dp, :, r, c], (to, head)).start()
            return carry

        lax.fori_loop(1, 8, step, 0)

    def spread_share(k):
        block = nc.at[(dp + 8 - k) % 8, :, :, c]
        return cols.copy(6 + k, block, block, core_dev)

    def collect(k, carry):
        cols.arrived(k - 1, nc.at[(dp + 8 - k) % 8, :, :, c], core_dev)
        spread_share(k).start()
        return carry

    def collected(k, carry):
        cols.arrived(6 + k, nc.at[(dp + 8 - k) % 8, :, :, 1 - c], core_dev)
        return carry

    def spread_sent(k, carry):
        to = (dp + k) % 8
        cols.copy(k - 1, xs.at[to, :, :, c], nc.at[dp, :, :, c], (to, head)).wait_send()
        spread_share(k).wait_send()
        return carry

    gx.on_pair()
    gg.start_pair()
    spread(z)
    gx.on_ring_own()
    gx.on_ring_pair()
    gg.start_ring()
    gg.on_pair()
    spread(gx.prv, gx.nxt)
    gx.on_far()
    gx.done(other_core(xs))

    for cp in weights[:3]:
        cp.wait()

    def project(ch, carry):
        block = xs[ch].reshape(SEQ, CHUNK)
        rows = pl.ds(pl.multiple_of(ch * CHUNK, CHUNK), CHUNK)
        acc[...] += dot(block, wq[rows, :])
        kvh_acc[...] += dot_nt(block, wkv[:, rows])
        return carry

    kvh_acc = probs.at[0, :, 0:HD]
    acc[...] = jnp.zeros_like(acc)
    kvh_acc[...] = jnp.zeros((SEQ, HD), F32)
    lax.fori_loop(0, CHUNKS, project, 0)
    kvh[c] = kvh_acc[...].astype(BF)
    kv_link = Link(kv_s, kv_r)
    kv_link.start(0, kvh.at[c], kvh.at[c], core_dev)
    spread(gx.far)
    gg.on_ring_own()
    for h in range(HEADS):
        pre = acc[:, h * HD : (h + 1) * HD].astype(BF).astype(F32)
        qh[h] = rope(pre).astype(BF)
    kv_link.arrived(0, kvh.at[1 - c], core_dev)
    first, second = kvh[0].astype(F32), kvh[1].astype(F32)
    key_pre = jnp.where(low_half, first, pltpu.roll(second, HD // 2, 1))
    values = jnp.where(low_half, pltpu.roll(first, HD // 2, 1), second).astype(BF)
    key_rows = rope(key_pre).astype(BF)
    score_scale = HD ** (-0.5)

    for h in range(HEADS):
        scores = dot_nt(qh[h], key_rows) * score_scale
        scores = jnp.where(allowed, scores, -1e30)
        top = jnp.max(scores, axis=-1, keepdims=True)
        e = jnp.exp(scores - top)
        p = e / jnp.sum(e, axis=-1, keepdims=True)
        probs[h] = p
        att[x, yh, :, h * HD : (h + 1) * HD] = dot(p.astype(BF), values).astype(BF)
    gat.start_ring()
    gat.start_pair()
    gg.on_ring_pair()

    weights[3].wait()
    wide = (2, 4, 2, ROWS, CHUNK)

    def project_out(ch):
        cols_ch = pl.ds(pl.multiple_of(ch * CHUNK, CHUNK), CHUNK)
        po[ch] = dot(att[x, yh], wo[:, cols_ch]).astype(BF).reshape(wide)
        ro.give_core(ch)

    ro.run(project_out)
    gg.on_far()
    for k in range(1, 8):
        tiny.arrived(k - 1, gc.at[(dp + 8 - k) % 8, yl, z, c, :, 0:CUT], core_dev)
    ggc.start_ring()
    ggc.start_pair()
    gat.on_pair()
    gg.done(other_core(gs))

    acc[...] = jnp.zeros_like(acc)

    def back_out(ch, carry):
        cols_ch = pl.ds(pl.multiple_of(ch * CHUNK, CHUNK), CHUNK)
        acc[...] += dot_nt(gs[ch].reshape(SEQ, CHUNK), wo[:, cols_ch])
        return carry

    lax.fori_loop(0, CHUNKS, back_out, 0)
    for ch in range(CHUNKS):
        ms[ch] = gs[ch, :, :, c, :, CUT:]
    for k in range(1, 8):
        to = (dp + k) % 8
        far_cols.start(k - 1, ms.at[to], gc.at[dp, :, :, c, :, CUT:], (to, head))
    gc[dp, :, :, :, :, CUT:] = gs[dp, :, :, :, :, CUT:]
    gat.on_ring_own()
    ggc.on_pair()
    key_sum = jnp.zeros((SEQ, HD), F32)
    value_sum = jnp.zeros((SEQ, HD), F32)
    for h in range(HEADS):
        grad_att = acc[:, h * HD : (h + 1) * HD].astype(BF)
        p = probs[h]
        grad_probs = dot_nt(grad_att, values)
        delta = jnp.sum(p * grad_probs, axis=-1, keepdims=True)
        grad_scores = (p * (grad_probs - delta)).astype(BF)
        grad_query = dot(grad_scores, key_rows) * score_scale
        qkv[x, yh, :, h * HD : (h + 1) * HD] = rope_back(grad_query).astype(BF)
        key_sum += dot_tn(grad_scores, qh[h])
        value_sum += dot_tn(p.astype(BF), grad_att)
    kvg[c, 0] = rope_back(key_sum * score_scale).astype(BF)
    kvg[c, 1] = value_sum.astype(BF)
    kv_link.start(1, kvg.at[c], kvg.at[c], core_dev)
    ro.middle()
    kv_link.arrived(1, kvg.at[1 - c], core_dev)
    key_pair = (kvg[0, 0].astype(F32) + kvg[1, 0].astype(F32)).astype(BF).astype(F32)
    value_pair = (kvg[0, 1].astype(F32) + kvg[1, 1].astype(F32)).astype(BF).astype(F32)
    even = jnp.where(low_half, key_pair, pltpu.roll(value_pair, HD // 2, 1))
    odd = jnp.where(low_half, pltpu.roll(key_pair, HD // 2, 1), value_pair)
    qkv[x, yh, :, HEADS * HD :] = jnp.where(c == 0, even, odd).astype(BF)
    gqk.start_ring()
    gqk.start_pair()
    gat.on_ring_pair()
    ggc.on_ring_own()
    gg.sent()
    tiny.sent()

    def back_in(ch):
        rows = pl.ds(pl.multiple_of(ch * CHUNK, CHUNK), CHUNK)
        part = dot_nt(qkv[x, yh, :, : HEADS * HD], wq[rows, :])
        part += dot(qkv[x, yh, :, HEADS * HD :], wkv[:, rows])
        gs[ch] = part.astype(BF).reshape(wide)
        rg.give_core(ch)

    rg.run(back_in)

    gain_slot = yl * 2 + c
    for ch in range(CHUNKS):
        term = gs[ch, :, :, c].astype(F32) * xs[ch, :, :, c].astype(F32)
        term = jnp.sum(term.reshape(SEQ // 2, CHUNK), axis=0, keepdims=True)
        ga0[gain_slot, ch : ch + 1] = term / gain_ref[:, ch * CHUNK : (ch + 1) * CHUNK]
    ga_link = Link(ga_s, ga_r)
    near = [(core_dev, yl * 2 + 1 - c), (pair_dev, (1 - yl) * 2 + c), (diag_dev, (1 - yl) * 2 + 1 - c)]
    for k, (to, _) in enumerate(near):
        ga_link.start(k, ga0.at[gain_slot], ga0.at[gain_slot], to)

    gqk.on_pair()
    gqk.on_ring_own()
    ro.to_pair()
    for k, (_, slot) in enumerate(near):
        ga_link.arrived(k, ga0.at[slot], core_dev)
    ga1[z] = (ga0[0] + ga0[1]) + (ga0[2] + ga0[3])
    for k in range(1, 4):
        ga_link.start(2 + k, ga1.at[z], ga1.at[z], z_dev[k])
    gat.on_far()
    rg.middle()
    ggc.on_ring_pair()
    nc[dp] = xs[dp]
    lax.fori_loop(1, 8, collect, 0)
    for h in range(2):
        ro.arrived(h)
        for ch in range(4 * h, 4 * h + 4):
            span = slice(ch * CHUNK, (ch + 1) * CHUNK)
            out_ref[:, span] = (inputs_ref[:, span].astype(F32) + ro.chunk(ch)).astype(BF)
    gqk.on_ring_pair()
    for k in range(1, 8):
        block = gc.at[(dp + 8 - k) % 8, :, :, c, :, CUT:]
        far_cols.arrived(k - 1, block, core_dev)
        far_cols.start(6 + k, block, block, core_dev)
    for k in range(1, 4):
        ga_link.arrived(2 + k, ga1.at[(z + 4 - k) % 4], core_dev)
    ga2[dp] = (ga1[0] + ga1[1]) + (ga1[2] + ga1[3])
    for k in range(1, 8):
        ga_link.start(5 + k, ga2.at[dp], ga2.at[dp], ((dp + k) % 8, head))

    lax.fori_loop(1, 8, collected, 0)
    early = [(a, b) for a in (x, gqk.prv, gqk.nxt) for b in (yh, 1 - yh)]
    late = [(gqk.far, yh), (gqk.far, 1 - yh)]
    rg.to_pair()
    ggc.on_far()
    for k in range(1, 8):
        ga_link.arrived(5 + k, ga2.at[(dp + 8 - k) % 8], core_dev)
    total = ((ga2[0] + ga2[1]) + (ga2[2] + ga2[3])) + ((ga2[4] + ga2[5]) + (ga2[6] + ga2[7]))
    for ch in range(CHUNKS):
        ggain_ref[:, ch * CHUNK : (ch + 1) * CHUNK] = total[ch : ch + 1]
    ggc.done(other_core(near_cols))
    for k in range(1, 8):
        far_cols.arrived(6 + k, gc.at[(dp + 8 - k) % 8, :, :, 1 - c, :, CUT:], core_dev)
    total = None
    for s in range(8):
        term = dot_tn(att[s // 2, s % 2], gc[s].reshape(SEQ, CHUNK))
        total = term if total is None else total + term
    gwo_ref[...] = total.astype(BF)

    total = None
    for a, b in early:
        term = dot_tn(nc[2 * a + b].reshape(SEQ, CHUNK), qkv[a, b])
        total = term if total is None else total + term
    mean = jnp.zeros((ROWS, 1), F32)
    for h in range(2):
        rg.arrived(h)
        for ch in range(4 * h, 4 * h + 4):
            span = slice(ch * CHUNK, (ch + 1) * CHUNK)
            part = inputs_ref[:, span].astype(F32)
            mean += jnp.sum(rg.chunk(ch) * gain_ref[:, span] * part, axis=-1, keepdims=True)
    mean = mean * (1.0 / (CHUNKS * CHUNK)) * inverse_rms * inverse_rms * inverse_rms
    for ch in range(CHUNKS):
        span = slice(ch * CHUNK, (ch + 1) * CHUNK)
        part = inputs_ref[:, span].astype(F32)
        scaled = rg.chunk(ch) * gain_ref[:, span]
        gin_ref[:, span] = (gout_ref[:, span].astype(F32) + inverse_rms * scaled - part * mean).astype(BF)
    gqk.on_far()
    for a, b in late:
        total += dot_tn(nc[2 * a + b].reshape(SEQ, CHUNK), qkv[a, b])
    gwq_ref[...] = total[:, : HEADS * HD].astype(BF)
    pairs = total[:, HEADS * HD :].T
    gwk_ref[...] = pairs[: HD // 2].astype(BF)
    gwv_ref[...] = pairs[HD // 2 :].astype(BF)
    lax.fori_loop(1, 8, spread_sent, 0)
    for link in (gx, gat, gqk, ggc, far_cols, ro, rg, kv_link, ga_link):
        link.sent()


def hand_over(*refs):
    src, dst, mid, sem_in, sem_out = refs[:7], refs[7:14], refs[14:21], refs[21], refs[22]
    loads = [pltpu.make_async_copy(src[i], mid[i], sem_in.at[i]) for i in range(7)]
    stores = [pltpu.make_async_copy(mid[i], dst[i], sem_out.at[i]) for i in range(7)]
    for cp in loads:
        cp.start()
    for load, store in zip(loads, stores):
        load.wait()
        store.start()
    for cp in stores:
        cp.wait()


def per_device(inputs, gain, doc_ids, w_query, w_key, w_value, w_out, grad_out):
    vmem = pl.BlockSpec(memory_space=pltpu.VMEM)
    hbm = pl.BlockSpec(memory_space=pl.ANY)
    rows = (CHUNKS, 2, 4, 2, ROWS, CHUNK)
    half = (4, 2, ROWS, CHUNK)
    scatter = [
        pltpu.VMEM((CHUNKS, 2, 4, ROWS, CHUNK), BF),
        pltpu.VMEM(half, BF),
        pltpu.VMEM(half, BF),
        pltpu.VMEM((CHUNKS, 2, ROWS, CHUNK), BF),
        pltpu.VMEM((CHUNKS, 2, ROWS, CHUNK), BF),
        pltpu.VMEM((CHUNKS, ROWS, CHUNK), BF),
    ]
    dma = lambda n: [pltpu.SemaphoreType.DMA((n,))] * 2
    outs = pl.pallas_call(
        layer,
        out_shape=(
            jax.ShapeDtypeStruct((ROWS, CHUNKS * CHUNK), BF),
            jax.ShapeDtypeStruct((ROWS, CHUNKS * CHUNK), BF),
            jax.ShapeDtypeStruct((1, CHUNKS * CHUNK), F32),
            jax.ShapeDtypeStruct((CHUNK, HEADS * HD), BF),
            jax.ShapeDtypeStruct((HD // 2, CHUNK), BF),
            jax.ShapeDtypeStruct((HD // 2, CHUNK), BF),
            jax.ShapeDtypeStruct((HEADS * HD, CHUNK), BF),
        ),
        in_specs=[vmem] * 3 + [hbm] * 4 + [vmem],
        out_specs=[vmem] * 7,
        scratch_shapes=[
            pltpu.VMEM(rows, BF),
            pltpu.VMEM(rows, BF),
            pltpu.VMEM(rows, BF),
            pltpu.VMEM(rows, BF),
            pltpu.VMEM(rows, BF),
            pltpu.VMEM((CHUNKS, 2, 4, ROWS, CHUNK - CUT), BF),
            pltpu.VMEM((CHUNKS * CHUNK, HEADS * HD), BF),
            pltpu.VMEM((HD, CHUNKS * CHUNK), BF),
            pltpu.VMEM((HEADS * HD, CHUNKS * CHUNK), BF),
            pltpu.VMEM((4, 2, SEQ, HEADS * HD), BF),
            pltpu.VMEM((4, 2, SEQ, HEADS * HD + HD), BF),
            pltpu.VMEM((SEQ, HEADS * HD), F32),
            pltpu.VMEM((2, SEQ, HD), BF),
            pltpu.VMEM((2, 2, SEQ, HD), BF),
            pltpu.VMEM((HEADS, SEQ, HD), BF),
            pltpu.VMEM((HEADS, SEQ, SEQ), F32),
        ]
        + scatter
        + scatter[1:]
        + [
            pltpu.VMEM((4, CHUNKS, CHUNK), F32),
            pltpu.VMEM((4, CHUNKS, CHUNK), F32),
            pltpu.VMEM((8, CHUNKS, CHUNK), F32),
        ]
        + dma(17) * 2
        + dma(14)
        + dma(17)
        + dma(14)
        + dma(9) * 2
        + dma(16) * 2
        + dma(7)
        + dma(2)
        + dma(13)
        + [pltpu.SemaphoreType.DMA((4,))],
        compiler_params=pltpu.CompilerParams(
            collective_id=0, has_side_effects=True, vmem_limit_bytes=62 * 2**20
        ),
    )(
        inputs,
        gain[None, :],
        doc_ids,
        w_query,
        w_key.T,
        w_value.T,
        w_out,
        grad_out,
    )
    out, gin, ggain, gwq, gwk, gwv, gwo = pl.pallas_call(
        hand_over,
        out_shape=[jax.ShapeDtypeStruct(o.shape, o.dtype) for o in outs],
        in_specs=[hbm] * 7,
        out_specs=[hbm] * 7,
        scratch_shapes=[pltpu.VMEM(o.shape, o.dtype) for o in outs] + dma(7),
    )(*outs)
    return (out, gin, ggain.reshape(-1), gwq, gwk.T, gwv.T, gwo)


def solution(mesh):
    return jax.shard_map(
        per_device,
        mesh=mesh,
        in_specs=(
            P(("dp", "head"), None),
            P(),
            P("dp", None),
            P(None, "head"),
            P(None, "head"),
            P(None, "head"),
            P("head", None),
            P(("dp", "head"), None),
        ),
        out_specs=(
            P(("dp", "head"), None),
            P(("dp", "head"), None),
            P(),
            P("dp", "head"),
            P("dp", "head"),
            P("dp", "head"),
            P("head", "dp"),
        ),
        check_vma=False,
    )
```

```python
import math

import jax
import jax.numpy as jnp
from jax import lax
from jax.experimental import pallas as pl
from jax.experimental.pallas import tpu as pltpu
from jax.sharding import PartitionSpec as P

EPSILON = 1e-05
LOG_THETA = math.log(500000.0)
MESH = pl.DeviceIdType.MESH
BF = jnp.bfloat16
F32 = jnp.float32

ROWS = 16
CHUNKS = 8
CHUNK = 1024
SEQ = 256
CUT = 768
HEADS = 4
HD = 128


def device(x, yh, yl, z, c):
    return (x * 2 + yh, (yl * 4 + z) * 2 + c)


def dot(a, b):
    return jnp.dot(a, b, preferred_element_type=F32)


def dot_nt(a, b):
    return lax.dot_general(a, b, (((1,), (1,)), ((), ())), preferred_element_type=F32)


def dot_tn(a, b):
    return lax.dot_general(a, b, (((0,), (0,)), ((), ())), preferred_element_type=F32)


class Link:
    def __init__(self, send, recv):
        self.send, self.recv, self.started = send, recv, []

    def copy(self, k, src, dst, to):
        return pltpu.make_async_remote_copy(
            src_ref=src,
            dst_ref=dst,
            send_sem=self.send.at[k],
            recv_sem=self.recv.at[k],
            device_id=to,
            device_id_type=MESH,
        )

    def start(self, k, src, dst, to):
        cp = self.copy(k, src, dst, to)
        cp.start()
        self.started.append(cp)

    def arrived(self, k, dst, to):
        self.copy(k, dst, dst, to).wait_recv()

    def sent(self):
        for cp in self.started:
            cp.wait_send()
        self.started = []


class Gather:
    def __init__(self, link, slot, half, place, pair, ring, core):
        self.link, self.slot, self.half = link, slot, half
        self.p, self.r = place
        self.pair_dev, self.core_dev = pair, core
        self.next_dev, self.prev_dev = ring
        self.q = 1 - self.p
        self.nxt, self.prv, self.far = (self.r + 1) % 4, (self.r + 3) % 4, (self.r + 2) % 4
        self.shared = []

    def put(self, k, p, r, to):
        ref = self.slot(p, r)
        self.link.start(k, ref, ref, to)

    def put_half(self, k, p, r, h, to):
        ref = self.half(p, r, h)
        self.link.start(k, ref, ref, to)

    def got(self, k, p, r):
        self.link.arrived(k, self.slot(p, r), self.pair_dev)

    def got_half(self, k, p, r, h):
        self.link.arrived(k, self.half(p, r, h), self.pair_dev)

    def share(self, p, r):
        if self.core_dev is not None:
            self.put(9 + len(self.shared), p, r, self.core_dev)
            self.shared.append((p, r))

    def start_pair(self):
        self.put(0, self.p, self.r, self.pair_dev)

    def start_ring(self):
        self.put(1, self.p, self.r, self.next_dev)
        self.put(2, self.p, self.r, self.prev_dev)
        self.share(self.p, self.r)

    def on_pair(self):
        self.got(0, self.q, self.r)
        self.put(3, self.q, self.r, self.next_dev)
        self.put(4, self.q, self.r, self.prev_dev)
        self.share(self.q, self.r)

    def on_ring(self, p, base, k):
        self.got(base, p, self.prv)
        self.put_half(k, p, self.prv, 0, self.next_dev)
        self.share(p, self.prv)
        self.got(base + 1, p, self.nxt)
        self.put_half(k + 1, p, self.nxt, 1, self.prev_dev)
        self.share(p, self.nxt)

    def on_ring_own(self):
        self.on_ring(self.p, 1, 5)

    def on_ring_pair(self):
        self.on_ring(self.q, 3, 7)

    def on_far(self):
        for p, k in ((self.p, 5), (self.q, 7)):
            self.got_half(k, p, self.far, 0)
            self.got_half(k + 1, p, self.far, 1)
            self.share(p, self.far)

    def last_ring(self):
        self.got(1, self.p, self.prv)
        self.put_half(5, self.p, self.prv, 0, self.next_dev)
        self.put(3, self.p, self.prv, self.pair_dev)
        self.share(self.p, self.prv)
        self.got(2, self.p, self.nxt)
        self.put_half(6, self.p, self.nxt, 1, self.prev_dev)
        self.put(4, self.p, self.nxt, self.pair_dev)
        self.share(self.p, self.nxt)

    def last_far(self):
        self.got_half(5, self.p, self.far, 0)
        self.got_half(6, self.p, self.far, 1)
        self.put(7, self.p, self.far, self.pair_dev)
        self.share(self.p, self.far)

    def last_pair(self):
        for k, r in ((0, self.r), (3, self.prv), (4, self.nxt), (7, self.far)):
            self.got(k, self.q, r)
            self.share(self.q, r)

    def done(self, other_slot=None):
        for i, (p, r) in enumerate(self.shared):
            self.link.arrived(9 + i, other_slot(p, r), self.pair_dev)

    def sent(self):
        self.link.sent()


class Scatter:
    def __init__(self, link, parts, bufs, place, devs):
        self.link, self.parts = link, parts
        self.from_core, self.from_prev_half, self.from_next_half, self.from_prev, self.from_next, self.from_pair = bufs
        self.yl, self.z, self.c = place
        self.core_dev, self.pair_dev, self.next_dev, self.prev_dev = devs
        self.nxt, self.prv, self.far = (self.z + 1) % 4, (self.z + 3) % 4, (self.z + 2) % 4

    def give_core(self, ch):
        self.link.copy(
            ch, self.parts.at[ch, :, :, 1 - self.c], self.from_core.at[ch], self.core_dev
        ).start()

    def add_core(self, ch):
        self.link.copy(
            ch, self.parts.at[ch, :, :, 1 - self.c], self.from_core.at[ch], self.core_dev
        ).wait()
        own = self.parts[ch, :, :, self.c].astype(F32)
        self.parts[ch, :, :, self.c] = (own + self.from_core[ch].astype(F32)).astype(BF)

    def run(self, make):
        half = CHUNKS // 2

        def first(ch, carry):
            make(ch)
            return carry

        def second(ch, carry):
            make(ch)
            self.add_core(ch - half)
            return carry

        def rest(ch, carry):
            self.add_core(ch)
            return carry

        lax.fori_loop(0, half, first, 0)
        lax.fori_loop(half, CHUNKS, second, 0)
        self.start_low()
        lax.fori_loop(half, CHUNKS, rest, 0)
        self.start_high()

    def half(self, z, h):
        return self.parts.at[4 * h : 4 * h + 4, :, z, self.c]

    def start_low(self):
        link = self.link
        link.start(8, self.half(self.far, 0), self.from_prev_half, self.next_dev)
        link.start(11, self.half(self.prv, 0), self.from_next.at[0:4], self.prev_dev)

    def start_high(self):
        link = self.link
        link.start(9, self.half(self.far, 1), self.from_next_half, self.prev_dev)
        link.start(10, self.half(self.nxt, 1), self.from_prev.at[4:8], self.next_dev)

    def middle(self):
        link = self.link
        link.arrived(8, self.from_prev_half, self.pair_dev)
        for ch in range(4):
            mine = self.parts[ch, :, self.nxt, self.c].astype(F32)
            self.parts[ch, :, self.nxt, self.c] = (mine + self.from_prev_half[ch].astype(F32)).astype(BF)
        link.start(12, self.half(self.nxt, 0), self.from_prev.at[0:4], self.next_dev)
        link.arrived(9, self.from_next_half, self.pair_dev)
        for ch in range(4):
            mine = self.parts[4 + ch, :, self.prv, self.c].astype(F32)
            self.parts[4 + ch, :, self.prv, self.c] = (mine + self.from_next_half[ch].astype(F32)).astype(BF)
        link.start(13, self.half(self.prv, 1), self.from_next.at[4:8], self.prev_dev)

    def to_pair(self):
        link = self.link
        link.arrived(10, self.from_prev.at[4:8], self.pair_dev)
        link.arrived(11, self.from_next.at[0:4], self.pair_dev)
        for k, h in ((12, 0), (13, 1)):
            buf = self.from_prev if h == 0 else self.from_next
            link.arrived(k, buf.at[4 * h : 4 * h + 4], self.pair_dev)
            for ch in range(4 * h, 4 * h + 4):
                total = (
                    self.parts[ch, :, self.z, self.c].astype(F32)
                    + self.from_prev[ch].astype(F32)
                    + self.from_next[ch].astype(F32)
                )
                self.parts[ch, :, self.z, self.c] = total.astype(BF)
            link.start(
                14 + h,
                self.parts.at[4 * h : 4 * h + 4, 1 - self.yl, self.z, self.c],
                self.from_pair.at[4 * h : 4 * h + 4],
                self.pair_dev,
            )

    def arrived(self, h):
        self.link.arrived(14 + h, self.from_pair.at[4 * h : 4 * h + 4], self.pair_dev)

    def chunk(self, ch):
        return self.parts[ch, self.yl, self.z, self.c].astype(F32) + self.from_pair[ch].astype(F32)

    def sent(self):
        self.link.sent()


def layer(
    inputs_ref, gain_ref, doc_ref, wq_hbm, wk_hbm, wv_hbm, wo_hbm, gout_ref,
    out_hbm, gin_hbm, ggain_hbm, gwq_hbm, gwk_hbm, gwv_hbm, gwo_hbm,
    out_ref, gin_ref, ggain_ref, gwq_ref, gwk_ref, gwv_ref, gwo_ref,
    xs, gs, nc, gc, po, ms, wq, wkv, wo, att, qkv, acc, kvh, kvg, qh, probs,
    rs0, rs1, rs2, rs3, rs4, rs5, rt1, rt2, rt3, rt4, rt5,
    ga0, ga1, ga2,
    x_s, x_r, g_s, g_r, nc_s, nc_r, gc_s, gc_r, fc_s, fc_r, at_s, at_r, qk_s, qk_r, ro_s, ro_r, rg_s, rg_r,
    tn_s, tn_r, kv_s, kv_r, ga_s, ga_r, w_sem, o_sem,
):
    dp, head = lax.axis_index("dp"), lax.axis_index("head")
    x, yh = dp // 2, dp % 2
    yl, z, c = head // 8, (head // 2) % 4, head % 2
    core_dev = device(x, yh, yl, z, 1 - c)
    pair_dev = device(x, yh, 1 - yl, z, c)
    z_dev = [device(x, yh, yl, (z + k) % 4, c) for k in range(4)]
    dp_devs = [((dp + k) % 8, head) for k in range(1, 8)]
    x_dev = [device((x + k) % 4, yh, yl, z, c) for k in range(4)]
    yh_dev = device(x, 1 - yh, yl, z, c)
    diag_dev = device(x, yh, 1 - yl, z, 1 - c)

    weights = [
        pltpu.make_async_copy(wq_hbm, wq, w_sem.at[0]),
        pltpu.make_async_copy(wk_hbm, wkv.at[0 : HD // 2], w_sem.at[1]),
        pltpu.make_async_copy(wv_hbm, wkv.at[HD // 2 : HD], w_sem.at[2]),
        pltpu.make_async_copy(wo_hbm, wo, w_sem.at[3]),
    ]
    for cp in weights:
        cp.start()

    results = [
        pltpu.make_async_copy(out_ref, out_hbm, o_sem.at[0]),
        pltpu.make_async_copy(gin_ref, gin_hbm, o_sem.at[1]),
        pltpu.make_async_copy(ggain_ref, ggain_hbm, o_sem.at[2]),
        pltpu.make_async_copy(gwq_ref, gwq_hbm, o_sem.at[3]),
        pltpu.make_async_copy(gwk_ref, gwk_hbm, o_sem.at[4]),
        pltpu.make_async_copy(gwv_ref, gwv_hbm, o_sem.at[5]),
        pltpu.make_async_copy(gwo_ref, gwo_hbm, o_sem.at[6]),
    ]
    barrier = pltpu.get_barrier_semaphore()
    partners = [core_dev, pair_dev, diag_dev] + z_dev[1:] + dp_devs
    for to in partners:
        pl.semaphore_signal(barrier, inc=1, device_id=to, device_id_type=MESH)

    square = jnp.zeros((ROWS, 1), F32)
    for ch in range(CHUNKS):
        part = inputs_ref[:, ch * CHUNK : (ch + 1) * CHUNK].astype(F32)
        square += jnp.sum(part * part, axis=-1, keepdims=True)
    inverse_rms = lax.rsqrt(square * (1.0 / (CHUNKS * CHUNK)) + EPSILON)
    for ch in range(CHUNKS):
        cols = slice(ch * CHUNK, (ch + 1) * CHUNK)
        part = inputs_ref[:, cols].astype(F32)
        xs[ch, yl, z, c] = (part * inverse_rms * gain_ref[:, cols]).astype(BF)
        gs[ch, yl, z, c] = gout_ref[:, cols]
    gc[dp, yl, z, c] = gs[dp, yl, z, c]

    pl.semaphore_wait(barrier, len(partners))

    def head_gather(buf, send, recv):
        return Gather(
            Link(send, recv),
            lambda p, r: buf.at[:, p, r, c],
            lambda p, r, h: buf.at[4 * h : 4 * h + 4, p, r, c],
            (yl, z), pair_dev, (z_dev[1], z_dev[3]), core_dev,
        )

    def other_core(buf):
        return lambda p, r: buf.at[:, p, r, 1 - c]

    def dp_gather(buf, send, recv):
        return Gather(
            Link(send, recv),
            lambda p, r: buf.at[r, p],
            lambda p, r, h: buf.at[r, p, 128 * h : 128 * h + 128],
            (yh, x), yh_dev, (x_dev[1], x_dev[3]), None,
        )

    gx, gg = head_gather(xs, x_s, x_r), head_gather(gs, g_s, g_r)
    near_cols = gc.at[:, :, :, :, :, 0:CUT]
    ggc = head_gather(near_cols, gc_s, gc_r)
    cols = Link(nc_s, nc_r)
    far_cols = Link(fc_s, fc_r)
    gat, gqk = dp_gather(att, at_s, at_r), dp_gather(qkv, qk_s, qk_r)
    devs = (core_dev, pair_dev, z_dev[1], z_dev[3])
    ro = Scatter(Link(ro_s, ro_r), po, (rs0, rs1, rs2, rs3, rs4, rs5), (yl, z, c), devs)
    rg = Scatter(Link(rg_s, rg_r), gs, (rs0, rt1, rt2, rt3, rt4, rt5), (yl, z, c), devs)

    gx.start_ring()
    gx.start_pair()
    tiny = Link(tn_s, tn_r)
    for k in range(1, 8):
        to = (dp + k) % 8
        tiny.start(k - 1, gs.at[to, yl, z, c, :, 0:CUT], gc.at[dp, yl, z, c, :, 0:CUT], (to, head))

    row_index = lax.broadcasted_iota(jnp.int32, (SEQ, SEQ), 0)
    col_index = lax.broadcasted_iota(jnp.int32, (SEQ, SEQ), 1)
    doc_rows = jnp.broadcast_to(doc_ref[...].astype(F32), (SEQ, SEQ))
    same = doc_rows == doc_rows.T
    allowed = same & (col_index <= row_index)
    position = jnp.sum(jnp.where(allowed, 1.0, 0.0), axis=-1, keepdims=True) - 1.0
    lane = lax.broadcasted_iota(jnp.int32, (SEQ, HD), 1)
    low_half = lane < HD // 2
    exponent = jnp.where(low_half, lane, lane - HD // 2).astype(F32) * (2.0 / HD)
    angles = position * jnp.exp(exponent * -LOG_THETA)
    cosine, sine = jnp.cos(angles), jnp.sin(angles)
    sine_turn = jnp.where(low_half, -sine, sine)

    def rope(u):
        return u * cosine + pltpu.roll(u, HD // 2, 1) * sine_turn

    def rope_back(g):
        turned = pltpu.roll(g * sine, HD // 2, 1)
        return g * cosine + jnp.where(low_half, turned, -turned)

    def spread(*places):
        def step(k, carry):
            to = (dp + k) % 8
            for r in places:
                cols.copy(k - 1, xs.at[to, :, r, c], nc.at[dp, :, r, c], (to, head)).start()
            return carry

        lax.fori_loop(1, 8, step, 0)

    def spread_share(k):
        block = nc.at[(dp + 8 - k) % 8, :, :, c]
        return cols.copy(6 + k, block, block, core_dev)

    def collect(k, carry):
        cols.arrived(k - 1, nc.at[(dp + 8 - k) % 8, :, :, c], core_dev)
        spread_share(k).start()
        return carry

    def collected(k, carry):
        cols.arrived(6 + k, nc.at[(dp + 8 - k) % 8, :, :, 1 - c], core_dev)
        return carry

    def spread_sent(k, carry):
        to = (dp + k) % 8
        cols.copy(k - 1, xs.at[to, :, :, c], nc.at[dp, :, :, c], (to, head)).wait_send()
        spread_share(k).wait_send()
        return carry

    gx.on_pair()
    gg.start_pair()
    spread(z)
    gx.on_ring_own()
    gx.on_ring_pair()
    gg.start_ring()
    gg.on_pair()
    spread(gx.prv, gx.nxt)
    gx.on_far()
    gx.done(other_core(xs))

    for cp in weights[:3]:
        cp.wait()

    def project(ch, carry):
        block = xs[ch].reshape(SEQ, CHUNK)
        rows = pl.ds(pl.multiple_of(ch * CHUNK, CHUNK), CHUNK)
        acc[...] += dot(block, wq[rows, :])
        kvh_acc[...] += dot_nt(block, wkv[:, rows])
        return carry

    kvh_acc = probs.at[0, :, 0:HD]
    acc[...] = jnp.zeros_like(acc)
    kvh_acc[...] = jnp.zeros((SEQ, HD), F32)
    lax.fori_loop(0, CHUNKS, project, 0)
    kvh[c] = kvh_acc[...].astype(BF)
    kv_link = Link(kv_s, kv_r)
    kv_link.start(0, kvh.at[c], kvh.at[c], core_dev)
    spread(gx.far)
    gg.on_ring_own()
    for h in range(HEADS):
        pre = acc[:, h * HD : (h + 1) * HD].astype(BF).astype(F32)
        qh[h] = rope(pre).astype(BF)
    kv_link.arrived(0, kvh.at[1 - c], core_dev)
    first, second = kvh[0].astype(F32), kvh[1].astype(F32)
    key_pre = jnp.where(low_half, first, pltpu.roll(second, HD // 2, 1))
    values = jnp.where(low_half, pltpu.roll(first, HD // 2, 1), second).astype(BF)
    key_rows = rope(key_pre).astype(BF)
    score_scale = HD ** (-0.5)

    for h in range(HEADS):
        scores = dot_nt(qh[h], key_rows) * score_scale
        scores = jnp.where(allowed, scores, -1e30)
        top = jnp.max(scores, axis=-1, keepdims=True)
        e = jnp.exp(scores - top)
        p = e / jnp.sum(e, axis=-1, keepdims=True)
        probs[h] = p
        att[x, yh, :, h * HD : (h + 1) * HD] = dot(p.astype(BF), values).astype(BF)
    gat.start_ring()
    gat.start_pair()
    gg.on_ring_pair()

    weights[3].wait()
    wide = (2, 4, 2, ROWS, CHUNK)

    def project_out(ch):
        cols_ch = pl.ds(pl.multiple_of(ch * CHUNK, CHUNK), CHUNK)
        po[ch] = dot(att[x, yh], wo[:, cols_ch]).astype(BF).reshape(wide)
        ro.give_core(ch)

    ro.run(project_out)
    gg.on_far()
    for k in range(1, 8):
        tiny.arrived(k - 1, gc.at[(dp + 8 - k) % 8, yl, z, c, :, 0:CUT], core_dev)
    ggc.start_ring()
    ggc.start_pair()
    gat.on_pair()
    gg.done(other_core(gs))

    acc[...] = jnp.zeros_like(acc)

    def back_out(ch, carry):
        cols_ch = pl.ds(pl.multiple_of(ch * CHUNK, CHUNK), CHUNK)
        acc[...] += dot_nt(gs[ch].reshape(SEQ, CHUNK), wo[:, cols_ch])
        return carry

    lax.fori_loop(0, CHUNKS, back_out, 0)
    for ch in range(CHUNKS):
        ms[ch] = gs[ch, :, :, c, :, CUT:]
    for k in range(1, 8):
        to = (dp + k) % 8
        far_cols.start(k - 1, ms.at[to], gc.at[dp, :, :, c, :, CUT:], (to, head))
    gc[dp, :, :, :, :, CUT:] = gs[dp, :, :, :, :, CUT:]
    gat.on_ring_own()
    ggc.on_pair()
    key_sum = jnp.zeros((SEQ, HD), F32)
    value_sum = jnp.zeros((SEQ, HD), F32)
    for h in range(HEADS):
        grad_att = acc[:, h * HD : (h + 1) * HD].astype(BF)
        p = probs[h]
        grad_probs = dot_nt(grad_att, values)
        delta = jnp.sum(p * grad_probs, axis=-1, keepdims=True)
        grad_scores = (p * (grad_probs - delta)).astype(BF)
        grad_query = dot(grad_scores, key_rows) * score_scale
        qkv[x, yh, :, h * HD : (h + 1) * HD] = rope_back(grad_query).astype(BF)
        key_sum += dot_tn(grad_scores, qh[h])
        value_sum += dot_tn(p.astype(BF), grad_att)
    kvg[c, 0] = rope_back(key_sum * score_scale).astype(BF)
    kvg[c, 1] = value_sum.astype(BF)
    kv_link.start(1, kvg.at[c], kvg.at[c], core_dev)
    ro.middle()
    kv_link.arrived(1, kvg.at[1 - c], core_dev)
    key_pair = (kvg[0, 0].astype(F32) + kvg[1, 0].astype(F32)).astype(BF).astype(F32)
    value_pair = (kvg[0, 1].astype(F32) + kvg[1, 1].astype(F32)).astype(BF).astype(F32)
    even = jnp.where(low_half, key_pair, pltpu.roll(value_pair, HD // 2, 1))
    odd = jnp.where(low_half, pltpu.roll(key_pair, HD // 2, 1), value_pair)
    qkv[x, yh, :, HEADS * HD :] = jnp.where(c == 0, even, odd).astype(BF)
    gqk.start_ring()
    gqk.start_pair()
    gat.on_ring_pair()
    ggc.on_ring_own()
    gg.sent()
    tiny.sent()

    def back_in(ch):
        rows = pl.ds(pl.multiple_of(ch * CHUNK, CHUNK), CHUNK)
        part = dot_nt(qkv[x, yh, :, : HEADS * HD], wq[rows, :])
        part += dot(qkv[x, yh, :, HEADS * HD :], wkv[:, rows])
        gs[ch] = part.astype(BF).reshape(wide)
        rg.give_core(ch)

    rg.run(back_in)

    gain_slot = yl * 2 + c
    for ch in range(CHUNKS):
        term = gs[ch, :, :, c].astype(F32) * xs[ch, :, :, c].astype(F32)
        term = jnp.sum(term.reshape(SEQ // 2, CHUNK), axis=0, keepdims=True)
        ga0[gain_slot, ch : ch + 1] = term / gain_ref[:, ch * CHUNK : (ch + 1) * CHUNK]
    ga_link = Link(ga_s, ga_r)
    near = [(core_dev, yl * 2 + 1 - c), (pair_dev, (1 - yl) * 2 + c), (diag_dev, (1 - yl) * 2 + 1 - c)]
    for k, (to, _) in enumerate(near):
        ga_link.start(k, ga0.at[gain_slot], ga0.at[gain_slot], to)

    gqk.on_pair()
    gqk.on_ring_own()
    ro.to_pair()
    for k, (_, slot) in enumerate(near):
        ga_link.arrived(k, ga0.at[slot], core_dev)
    ga1[z] = (ga0[0] + ga0[1]) + (ga0[2] + ga0[3])
    for k in range(1, 4):
        ga_link.start(2 + k, ga1.at[z], ga1.at[z], z_dev[k])
    gat.on_far()
    rg.middle()
    ggc.on_ring_pair()
    nc[dp] = xs[dp]
    lax.fori_loop(1, 8, collect, 0)
    for h in range(2):
        ro.arrived(h)
        for ch in range(4 * h, 4 * h + 4):
            span = slice(ch * CHUNK, (ch + 1) * CHUNK)
            out_ref[:, span] = (inputs_ref[:, span].astype(F32) + ro.chunk(ch)).astype(BF)
    results[0].start()
    gqk.on_ring_pair()
    for k in range(1, 8):
        block = gc.at[(dp + 8 - k) % 8, :, :, c, :, CUT:]
        far_cols.arrived(k - 1, block, core_dev)
        far_cols.start(6 + k, block, block, core_dev)
    for k in range(1, 4):
        ga_link.arrived(2 + k, ga1.at[(z + 4 - k) % 4], core_dev)
    ga2[dp] = (ga1[0] + ga1[1]) + (ga1[2] + ga1[3])
    for k in range(1, 8):
        ga_link.start(5 + k, ga2.at[dp], ga2.at[dp], ((dp + k) % 8, head))

    lax.fori_loop(1, 8, collected, 0)
    early = [(a, b) for a in (x, gqk.prv, gqk.nxt) for b in (yh, 1 - yh)]
    late = [(gqk.far, yh), (gqk.far, 1 - yh)]
    rg.to_pair()
    ggc.on_far()
    for k in range(1, 8):
        ga_link.arrived(5 + k, ga2.at[(dp + 8 - k) % 8], core_dev)
    total = ((ga2[0] + ga2[1]) + (ga2[2] + ga2[3])) + ((ga2[4] + ga2[5]) + (ga2[6] + ga2[7]))
    for ch in range(CHUNKS):
        ggain_ref[:, ch * CHUNK : (ch + 1) * CHUNK] = total[ch : ch + 1]
    results[2].start()
    ggc.done(other_core(near_cols))
    for k in range(1, 8):
        far_cols.arrived(6 + k, gc.at[(dp + 8 - k) % 8, :, :, 1 - c, :, CUT:], core_dev)
    total = None
    for s in range(8):
        term = dot_tn(att[s // 2, s % 2], gc[s].reshape(SEQ, CHUNK))
        total = term if total is None else total + term
    gwo_ref[...] = total.astype(BF)
    results[6].start()

    total = None
    for a, b in early:
        term = dot_tn(nc[2 * a + b].reshape(SEQ, CHUNK), qkv[a, b])
        total = term if total is None else total + term
    mean = jnp.zeros((ROWS, 1), F32)
    for h in range(2):
        rg.arrived(h)
        for ch in range(4 * h, 4 * h + 4):
            span = slice(ch * CHUNK, (ch + 1) * CHUNK)
            part = inputs_ref[:, span].astype(F32)
            mean += jnp.sum(rg.chunk(ch) * gain_ref[:, span] * part, axis=-1, keepdims=True)
    mean = mean * (1.0 / (CHUNKS * CHUNK)) * inverse_rms * inverse_rms * inverse_rms
    for ch in range(CHUNKS):
        span = slice(ch * CHUNK, (ch + 1) * CHUNK)
        part = inputs_ref[:, span].astype(F32)
        scaled = rg.chunk(ch) * gain_ref[:, span]
        gin_ref[:, span] = (gout_ref[:, span].astype(F32) + inverse_rms * scaled - part * mean).astype(BF)
    results[1].start()
    gqk.on_far()
    for a, b in late:
        total += dot_tn(nc[2 * a + b].reshape(SEQ, CHUNK), qkv[a, b])
    gwq_ref[...] = total[:, : HEADS * HD].astype(BF)
    results[3].start()
    pairs = total[:, HEADS * HD :].T
    gwk_ref[...] = pairs[: HD // 2].astype(BF)
    gwv_ref[...] = pairs[HD // 2 :].astype(BF)
    results[4].start()
    results[5].start()
    lax.fori_loop(1, 8, spread_sent, 0)
    for link in (gx, gat, gqk, ggc, far_cols, ro, rg, kv_link, ga_link):
        link.sent()
    for cp in results:
        cp.wait()


def hand_over(*refs):
    src, dst, mid, sem_in, sem_out = refs[:7], refs[7:14], refs[14:21], refs[21], refs[22]
    parts = []
    for i in (3, 6, 0, 1, 4, 5, 2):
        rows = src[i].shape[0]
        step = rows // 2 if rows >= 256 else rows
        parts += [(i, slice(low, low + step)) for low in range(0, rows, step)]
    loads = [
        pltpu.make_async_copy(src[i].at[rows], mid[i].at[rows], sem_in.at[n])
        for n, (i, rows) in enumerate(parts)
    ]
    stores = [
        pltpu.make_async_copy(mid[i].at[rows], dst[i].at[rows], sem_out.at[n])
        for n, (i, rows) in enumerate(parts)
    ]
    for cp in loads:
        cp.start()
    for load, store in zip(loads, stores):
        load.wait()
        store.start()
    for cp in stores:
        cp.wait()


def per_device(inputs, gain, doc_ids, w_query, w_key, w_value, w_out, grad_out):
    vmem = pl.BlockSpec(memory_space=pltpu.VMEM)
    hbm = pl.BlockSpec(memory_space=pl.ANY)
    rows = (CHUNKS, 2, 4, 2, ROWS, CHUNK)
    half = (4, 2, ROWS, CHUNK)
    scatter = [
        pltpu.VMEM((CHUNKS, 2, 4, ROWS, CHUNK), BF),
        pltpu.VMEM(half, BF),
        pltpu.VMEM(half, BF),
        pltpu.VMEM((CHUNKS, 2, ROWS, CHUNK), BF),
        pltpu.VMEM((CHUNKS, 2, ROWS, CHUNK), BF),
        pltpu.VMEM((CHUNKS, ROWS, CHUNK), BF),
    ]
    dma = lambda n: [pltpu.SemaphoreType.DMA((n,))] * 2
    results = (
        jax.ShapeDtypeStruct((ROWS, CHUNKS * CHUNK), BF),
        jax.ShapeDtypeStruct((ROWS, CHUNKS * CHUNK), BF),
        jax.ShapeDtypeStruct((1, CHUNKS * CHUNK), F32),
        jax.ShapeDtypeStruct((CHUNK, HEADS * HD), BF),
        jax.ShapeDtypeStruct((HD // 2, CHUNK), BF),
        jax.ShapeDtypeStruct((HD // 2, CHUNK), BF),
        jax.ShapeDtypeStruct((HEADS * HD, CHUNK), BF),
    )
    outs = pl.pallas_call(
        layer,
        out_shape=results,
        in_specs=[vmem] * 3 + [hbm] * 4 + [vmem],
        out_specs=[hbm] * 7,
        scratch_shapes=[pltpu.VMEM(o.shape, o.dtype) for o in results]
        + [
            pltpu.VMEM(rows, BF),
            pltpu.VMEM(rows, BF),
            pltpu.VMEM(rows, BF),
            pltpu.VMEM(rows, BF),
            pltpu.VMEM(rows, BF),
            pltpu.VMEM((CHUNKS, 2, 4, ROWS, CHUNK - CUT), BF),
            pltpu.VMEM((CHUNKS * CHUNK, HEADS * HD), BF),
            pltpu.VMEM((HD, CHUNKS * CHUNK), BF),
            pltpu.VMEM((HEADS * HD, CHUNKS * CHUNK), BF),
            pltpu.VMEM((4, 2, SEQ, HEADS * HD), BF),
            pltpu.VMEM((4, 2, SEQ, HEADS * HD + HD), BF),
            pltpu.VMEM((SEQ, HEADS * HD), F32),
            pltpu.VMEM((2, SEQ, HD), BF),
            pltpu.VMEM((2, 2, SEQ, HD), BF),
            pltpu.VMEM((HEADS, SEQ, HD), BF),
            pltpu.VMEM((HEADS, SEQ, SEQ), F32),
        ]
        + scatter
        + scatter[1:]
        + [
            pltpu.VMEM((4, CHUNKS, CHUNK), F32),
            pltpu.VMEM((4, CHUNKS, CHUNK), F32),
            pltpu.VMEM((8, CHUNKS, CHUNK), F32),
        ]
        + dma(17) * 2
        + dma(14)
        + dma(17)
        + dma(14)
        + dma(9) * 2
        + dma(16) * 2
        + dma(7)
        + dma(2)
        + dma(13)
        + [pltpu.SemaphoreType.DMA((4,)), pltpu.SemaphoreType.DMA((7,))],
        compiler_params=pltpu.CompilerParams(
            collective_id=0, has_side_effects=True, vmem_limit_bytes=62 * 2**20
        ),
    )(
        inputs,
        gain[None, :],
        doc_ids,
        w_query,
        w_key.T,
        w_value.T,
        w_out,
        grad_out,
    )
    out, gin, ggain, gwq, gwk, gwv, gwo = pl.pallas_call(
        hand_over,
        out_shape=[jax.ShapeDtypeStruct(o.shape, o.dtype) for o in outs],
        in_specs=[hbm] * 7,
        out_specs=[hbm] * 7,
        scratch_shapes=[pltpu.VMEM(o.shape, o.dtype) for o in outs] + dma(9),
    )(*outs)
    return (out, gin, ggain.reshape(-1), gwq, gwk.T, gwv.T, gwo)


def solution(mesh):
    return jax.shard_map(
        per_device,
        mesh=mesh,
        in_specs=(
            P(("dp", "head"), None),
            P(),
            P("dp", None),
            P(None, "head"),
            P(None, "head"),
            P(None, "head"),
            P("head", None),
            P(("dp", "head"), None),
        ),
        out_specs=(
            P(("dp", "head"), None),
            P(("dp", "head"), None),
            P(),
            P("dp", "head"),
            P("dp", "head"),
            P("dp", "head"),
            P("head", "dp"),
        ),
        check_vma=False,
    )
```
